512 devices in a mesh: branch: 8 (over z_lo), tok: 64 (over y, z_hi, x, core).
Axes of the slice: x: 4, y: 4, z: 16 (z_hi: 2, z_lo: 8; z = z_hi * 8 + z_lo), core: 2. Of those that a mesh axis runs over, the one named last changes fastest.
Arguments:
- teacher_hidden: bfloat16 [8, 1024, 4096], P('branch', 'tok'), may hold values from -400 to 400
- teacher_gain: float32 [8, 4096], P('branch'), may hold values from 0.5 to 1.5
- teacher_head: bfloat16 [8, 4096, 20480], P('branch', None, 'tok'), may hold values from -30 to 30
- student_hidden: bfloat16 [1024, 4096], P('branch'), may hold values from -400 to 400
- student_gain: float32 [4096], replicated, may hold values from 0.5 to 1.5
- student_head: bfloat16 [4096, 20480], P('branch', 'tok'), may hold values from -30 to 30
- cluster_weights: int32 [1024, 8], P(None, 'branch'), may hold values from 0 to 64, as said below
- token_ids: int32 [1024], P('branch'), may hold values from 0 to 20479
Outputs:
- grad_head: float32 [4096, 20480], P('branch', 'tok')
- grad_hidden: float32 [1024, 4096], P('branch', 'tok')
- grad_gain: float32 [4096], P('tok')
The draws below stay inside these ranges and needn't reach their ends.
Inputs may be any that keep to these rules, and one draw needn't show every extreme that they name: `cluster_weights`: each token's 8 weights sum to 64.
All inputs are finite; a program needn't handle non-finite values.
Results may differ from the reference program's by a relative error of at most 0.0063.
Values may be sent and summed in bfloat16 or wider, within the bound.
A program may use at most 64 MiB of HBM per device.

```python
import math
import jax
import jax.numpy as jnp
import numpy as np
from jax import lax

D = 4096
V = 20480
DEN = 64
BRANCHES = 8
TOKENS = 1024


def column_sigma():
    position = jnp.arange(V, dtype=jnp.float32) / V
    return 2.6 + 0.8 * position


def make_pair(key):
    keys = jax.random.split(key, 4)
    width_root = jnp.sqrt(jnp.float32(D))
    head = jax.random.truncated_normal(keys[0], -4.0, 4.0, (D, V), jnp.float32) * column_sigma()[None, :] / width_root
    row_spread = jnp.exp(jax.random.uniform(keys[1], (TOKENS, 1), jnp.float32) * jnp.log(10.0))
    col_spread = jnp.exp(jax.random.uniform(keys[2], (1, D), jnp.float32) * jnp.log(10.0))
    hidden = jax.random.truncated_normal(keys[3], -4.0, 4.0, (TOKENS, D), jnp.float32) * row_spread * col_spread
    return (head, hidden)


def draw_teacher_head(key, part):
    seed_base = jax.random.fold_in(key, 101)
    return lax.map(lambda branch_index: make_pair(jax.random.fold_in(seed_base, branch_index))[0], jnp.arange(BRANCHES)).astype(jnp.bfloat16)


def draw_teacher_hidden(key, part):
    seed_base = jax.random.fold_in(key, 101)
    return lax.map(lambda branch_index: make_pair(jax.random.fold_in(seed_base, branch_index))[1], jnp.arange(BRANCHES)).astype(jnp.bfloat16)


def draw_student_head(key, part):
    return make_pair(jax.random.fold_in(key, 202))[0].astype(jnp.bfloat16)


def draw_student_hidden(key, part):
    return make_pair(jax.random.fold_in(key, 202))[1].astype(jnp.bfloat16)


def draw_cluster_weights(key, part):
    cuts = jnp.sort(jax.random.randint(jax.random.fold_in(key, 303), (TOKENS, BRANCHES - 1), 0, DEN + 1), axis=1)
    single = jax.random.randint(jax.random.fold_in(key, 304), (), 0, TOKENS)
    rows = jnp.arange(TOKENS, dtype=jnp.int32)[:, None]
    cuts = jnp.where(rows == single, jnp.zeros_like(cuts), cuts)
    edges = jnp.concatenate([jnp.zeros((TOKENS, 1), jnp.int32), cuts.astype(jnp.int32), jnp.full((TOKENS, 1), DEN, jnp.int32)], axis=1)
    return (edges[:, 1:] - edges[:, :-1]).astype(jnp.int32)


def set_ends(array, rng, least, high):
    longest = array.shape.index(max(array.shape))
    spots = []
    for shift in (0, 1):
        where = [jax.random.randint(jax.random.fold_in(rng, axis), (), 0, length) for axis, length in enumerate(array.shape)]
        where[longest] = (where[longest] + shift) % array.shape[longest]
        spots.append(tuple(where))
    return array.at[spots[0]].set(least).at[spots[1]].set(high)


def cumulative_ranks(number_of, skew):
    loads = [(1 << 20) // math.isqrt(rank ** skew) + 1 for rank in range(1, number_of + 1)]
    width = 1 + sum(loads) // (1 << 30)
    return np.cumsum(np.array([max(1, weight // width) for weight in loads]))


def skewed_ids(own_key, dims, amount, lean):
    grid = cumulative_ranks(amount, lean)
    ticket = jax.random.randint(jax.random.fold_in(own_key, 1), dims, 0, int(grid[amount - 1]))
    grade = jnp.searchsorted(jnp.asarray(grid, jnp.int32), ticket, side="right")
    return jax.random.permutation(jax.random.fold_in(own_key, 2), amount)[grade].astype(jnp.int32)


def setup_inputs(seed: int = 0) -> dict:
    key_list = jax.random.split(jax.random.key(seed), 9)
    return {
        "teacher_hidden": draw_teacher_hidden(jax.random.fold_in(key_list[8], 71), 0),
        "teacher_gain": jnp.clip(1.0 + 0.1 * jax.random.normal(key_list[1], (BRANCHES, D), jnp.float32), 0.5, 1.5),
        "teacher_head": draw_teacher_head(jax.random.fold_in(key_list[8], 71), 0),
        "student_hidden": draw_student_hidden(jax.random.fold_in(key_list[8], 71), 0),
        "student_gain": jnp.clip(1.0 + 0.1 * jax.random.normal(key_list[4], (D,), jnp.float32), 0.5, 1.5),
        "student_head": draw_student_head(jax.random.fold_in(key_list[8], 71), 0),
        "cluster_weights": draw_cluster_weights(jax.random.fold_in(key_list[8], 71), 0),
        "token_ids": set_ends(skewed_ids(key_list[7], (TOKENS,), V, 2), jax.random.fold_in(key_list[7], 3), 0, V - 1).astype(jnp.int32),
    }


eps = 1e-05
mix_label = 0.25
loss_scale = 64.0

def normalize(hidden, gain):
    values = hidden.astype(jnp.float32)
    inv_scale = lax.rsqrt(lax.optimization_barrier(jnp.mean(values * values, axis=-1, keepdims=True)) + eps)
    return ((values * inv_scale * gain.astype(jnp.float32)).astype(jnp.bfloat16), inv_scale)

def softmax_rows(logits):
    top = lax.optimization_barrier(jnp.max(logits, axis=-1, keepdims=True))
    scaled = jnp.exp(logits - top)
    return scaled / lax.optimization_barrier(jnp.sum(scaled, axis=-1, keepdims=True))

def reference(teacher_hidden, teacher_gain, teacher_head, student_hidden, student_gain, student_head, cluster_weights, token_ids):
    mixed = jnp.zeros((TOKENS, V), jnp.float32)
    for branch_index in range(BRANCHES):
        normed, unused_scale = normalize(teacher_hidden[branch_index], teacher_gain[branch_index])
        logits = jnp.dot(normed, teacher_head[branch_index], preferred_element_type=jnp.float32)
        weight = cluster_weights[:, branch_index].astype(jnp.float32) / DEN
        mixed = mixed + softmax_rows(logits) * weight[:, None]
    onehot = (token_ids[:, None] == jnp.arange(V, dtype=jnp.int32)[None, :]).astype(jnp.float32)
    targets = (1.0 - mix_label) * mixed + mix_label * onehot
    student_normed, inv_scale = normalize(student_hidden, student_gain)
    student_probs = softmax_rows(jnp.dot(student_normed, student_head, preferred_element_type=jnp.float32))
    logit_grads = (loss_scale * (student_probs - targets)).astype(jnp.bfloat16)
    grad_head = jnp.dot(student_normed.T, logit_grads, preferred_element_type=jnp.float32)
    normed_grads = jnp.dot(logit_grads, student_head.T, preferred_element_type=jnp.float32)
    values = student_hidden.astype(jnp.float32)
    gain = student_gain.astype(jnp.float32)
    grad_gain = lax.optimization_barrier(jnp.sum(normed_grads * values * inv_scale, axis=0))
    row_dots = lax.optimization_barrier(jnp.sum(gain[None, :] * normed_grads * values, axis=1, keepdims=True))
    grad_hidden = inv_scale * gain[None, :] * normed_grads - values * inv_scale ** 3 * row_dots / D
    return (grad_head, grad_hidden, grad_gain)
```

```python
import jax
import jax.numpy as jnp
from jax import lax
from jax.experimental import pallas as pl
from jax.experimental.pallas import tpu as pltpu
from jax.sharding import Mesh
from jax.sharding import PartitionSpec as P

DEN = 64
Y, H, X, C = "tok_0", "tok_1", "tok_2", "tok_3"
TOK = (Y, H, X, C)
MESH = pl.DeviceIdType.MESH


def ring(value, step, size):
    return lax.rem(value + (step + size), size)


def gather_kernel(block_ref, out_ref, local_sem, send_sem, recv_sem):
    y, h, x, c = (lax.axis_index(name) for name in TOK)
    width = block_ref.shape[1]
    half = width // 2
    barrier = pltpu.get_barrier_semaphore()
    peers = (
        {X: ring(x, 1, 4)}, {X: ring(x, -1, 4)}, {Y: ring(y, 1, 4)}, {Y: ring(y, -1, 4)},
        {H: 1 - h}, {C: 1 - c},
    )
    for peer in peers:
        pl.semaphore_signal(barrier, inc=1, device_id=peer, device_id_type=MESH)
    pl.semaphore_wait(barrier, len(peers))

    numbers = iter(range(64))
    sent = []

    def move(piece, peer, arriving, first=None):
        number = next(numbers)
        copy = pltpu.make_async_remote_copy(
            src_ref=piece if first is None else first, dst_ref=piece, send_sem=send_sem.at[number],
            recv_sem=recv_sem.at[number], device_id=peer, device_id_type=MESH,
        )
        copy.start()
        sent.append(copy)
        incoming = pltpu.make_async_remote_copy(
            src_ref=arriving, dst_ref=arriving, send_sem=send_sem.at[number],
            recv_sem=recv_sem.at[number], device_id=peer, device_id_type=MESH,
        )
        return incoming.wait_recv

    def blocks(ys, hs, xs, core, cols):
        return out_ref.at[ys, hs, xs, core, :, cols]

    own = pltpu.make_async_copy(block_ref, out_ref.at[y, h, x, c], local_sem)
    own.start()
    everything = pl.ds(0, width)
    across = move(blocks(y, h, x, c, everything), {H: 1 - h}, blocks(y, 1 - h, x, c, everything), block_ref)
    last = []

    def route(side, plane, fresh):
        start = side * half
        cols = pl.ds(start, half)
        quarters = (pl.ds(start, half // 2), pl.ds(start + half // 2, half // 2))
        axis, other = ((X, Y), (Y, X))[side]
        mine, theirs = ((x, y), (y, x))[side]

        def near(step, cs):
            at = ring(mine, step, 4)
            return blocks(y, plane, at, c, cs) if side == 0 else blocks(at, plane, x, c, cs)

        def rows(step, core, cs):
            at = ring(theirs, step, 4)
            every = pl.ds(0, 4)
            return blocks(at, plane, every, core, cs) if side == 0 else blocks(every, plane, at, core, cs)

        def to(name, step):
            return {name: ring(mine if name == axis else theirs, step, 4)}

        def share(step):
            last.append(move(rows(step, c, cols), {C: 1 - c}, rows(step, 1 - c, cols)))

        first = block_ref.at[:, cols] if fresh else None
        up = move(near(0, cols), to(axis, 1), near(-1, cols), first)
        down = move(near(0, cols), to(axis, -1), near(1, cols), first)
        yield
        up()
        far_up = move(near(-1, quarters[0]), to(axis, 1), near(2, quarters[0]))
        down()
        far_down = move(near(1, quarters[1]), to(axis, -1), near(2, quarters[1]))
        yield
        far_up()
        far_down()
        up = move(rows(0, c, cols), to(other, 1), rows(-1, c, cols))
        down = move(rows(0, c, cols), to(other, -1), rows(1, c, cols))
        share(0)
        yield
        up()
        far_up = move(rows(-1, c, quarters[0]), to(other, 1), rows(2, c, quarters[0]))
        down()
        far_down = move(rows(1, c, quarters[1]), to(other, -1), rows(2, c, quarters[1]))
        share(-1)
        share(1)
        yield
        far_up()
        far_down()
        share(2)

    routes = [route(0, h, True), route(1, h, True)]
    for turn in range(4):
        if turn == 2:
            own.wait()
        for r in routes:
            next(r)
    across()
    late = [route(0, 1 - h, False), route(1, 1 - h, False)]
    for r in late:
        next(r)
    for r in routes:
        next(r, None)
    for _ in range(4):
        for r in late:
            next(r, None)
    for arrive in last:
        arrive()
    for copy in sent:
        copy.wait_send()


def gather_tokens(block):
    rows, width = block.shape
    out = pl.pallas_call(
        gather_kernel,
        out_shape=jax.ShapeDtypeStruct((4, 2, 4, 2, rows, width), block.dtype),
        in_specs=[pl.BlockSpec(memory_space=pl.ANY)],
        out_specs=pl.BlockSpec(memory_space=pl.ANY),
        scratch_shapes=[
            pltpu.SemaphoreType.DMA,
            pltpu.SemaphoreType.DMA((64,)),
            pltpu.SemaphoreType.DMA((64,)),
        ],
        compiler_params=pltpu.CompilerParams(collective_id=0, has_side_effects=True),
        name="gather_tokens",
    )(block)
    return out.reshape(64 * rows, width)


eps = 1e-05
mix_label = 0.25
loss_scale = 64.0


def copy_for_each(value, axis):
    copies = jnp.broadcast_to(value, (lax.axis_size(axis), *value.shape))
    return lax.all_to_all(copies, axis, split_axis=0, concat_axis=0, tiled=True)


def collected_together(value, axis):
    leaves = jax.tree.leaves(value)
    turns = sorted(range(len(leaves)), key=lambda k: -leaves[k].size)
    width = (1, *leaves[turns[0]].shape)[-1]
    lines = [
        jnp.pad(leaves[k].reshape(-1), (0, -leaves[k].size % width)).reshape(-1, width)
        for k in turns
    ]
    both, at, found = (copy_for_each(jnp.concatenate(lines), axis), 0, {})
    for k, line in zip(turns, lines):
        slab = both[:, at : at + len(line)].reshape(len(both), -1)
        found[k] = slab[:, : leaves[k].size].reshape(-1, *leaves[k].shape)
        at += len(line)
    numbers = iter(range(len(leaves)))
    return jax.tree.map(lambda _: found[next(numbers)], value)


def joined_by_halves(pieces, combine):
    while len(jax.tree.leaves(pieces)[0]) > 1:
        pieces = jax.vmap(combine)(
            *(jax.tree.map(lambda part: part[side::2], pieces) for side in (0, 1))
        )
    return jax.tree.map(lambda part: part[0], pieces)


def joined_all(value, axis, combine):
    pieces = collected_together(value, axis)
    return joined_by_halves(pieces, combine)


def cut_along(value, dim, size):
    dims = value.shape
    blocks = value.reshape(*dims[:dim], size, dims[dim] // size, *dims[dim + 1 :])
    return jnp.moveaxis(blocks, dim, 0)


def summed_on_arrival(value, axis, dim):
    blocks = cut_along(value, dim, lax.axis_size(axis))
    arrived = lax.all_to_all(blocks, axis, split_axis=0, concat_axis=0, tiled=True)
    return arrived.sum(axis=0)


def in_order(blocks, dim):
    dims = list(blocks.shape[1:])
    dims[dim] *= blocks.shape[0]
    return jnp.moveaxis(blocks, 0, dim).reshape(dims)


def gathered_copies(value, axis, dim):
    blocks = copy_for_each(value, axis)
    return in_order(blocks, dim)


def summed_rows(value, axes, dim):
    far, near = axes
    blocks = cut_along(value, dim, lax.axis_size(far))
    nearer = summed_on_arrival(blocks, near, dim + 1)
    arrived = lax.all_to_all(nearer, far, split_axis=0, concat_axis=0, tiled=True)
    return arrived.sum(axis=0)


def over_copies(value, axis):
    everything = copy_for_each(value, axis)
    return jnp.sum(everything, axis=0)


def normalize(hidden, gain):
    values = hidden.astype(jnp.float32)
    inv_scale = lax.rsqrt(jnp.mean(values * values, axis=-1, keepdims=True) + eps)
    return ((values * inv_scale * gain).astype(jnp.bfloat16), inv_scale)


def combine_stats(first, second):
    top = jnp.maximum(first[0], second[0])
    return (top, first[1] * jnp.exp(first[0] - top) + second[1] * jnp.exp(second[0] - top))


def probabilities(logits):
    local_max = jnp.max(logits, axis=1)
    local_scaled = jnp.exp(logits - local_max[:, None])
    row_max, row_total = joined_all((local_max, jnp.sum(local_scaled, axis=1)), TOK, combine_stats)
    scaled = local_scaled * jnp.exp(local_max - row_max)[:, None]
    return scaled / row_total[:, None]


def per_device(
    teacher_hidden,
    teacher_gain,
    teacher_head,
    student_hidden,
    student_gain,
    student_head,
    cluster_weights,
    token_ids,
):
    width = student_hidden.shape[1]
    head_cols = teacher_head.shape[2]
    branch_gain = teacher_gain[0]
    branch_head = teacher_head[0]
    own_normed, unused_scale = normalize(teacher_hidden[0], branch_gain)
    normed = gather_tokens(own_normed)
    teacher_logits = jnp.dot(normed, branch_head, preferred_element_type=jnp.float32)
    weight = cluster_weights[:, 0].astype(jnp.float32) / DEN
    terms = probabilities(teacher_logits) * weight[:, None]
    mixed = summed_on_arrival(terms, "branch", 0)
    student_normed, inv_scale = normalize(student_hidden, student_gain)
    whole_head = gathered_copies(student_head, "branch", 0)
    student_logits = jnp.dot(student_normed, whole_head, preferred_element_type=jnp.float32)
    student_probs = probabilities(student_logits)
    offset = lax.axis_index(TOK) * head_cols
    onehot = (
        token_ids[:, None] == offset + jnp.arange(head_cols, dtype=jnp.int32)[None, :]
    ).astype(jnp.float32)
    targets = (1.0 - mix_label) * mixed + mix_label * onehot
    logit_grads = (loss_scale * (student_probs - targets)).astype(jnp.bfloat16)
    contract = (((1,), (1,)), ((), ()))
    partial_grads = lax.dot_general(
        logit_grads, whole_head, contract, preferred_element_type=jnp.float32
    )
    normed_grads = summed_rows(partial_grads, (("tok_0", "tok_1", "tok_2"), "tok_3"), 1)
    slice_width = normed_grads.shape[1]
    col_start = lax.axis_index(TOK) * slice_width
    hidden_cols = lax.dynamic_slice_in_dim(student_hidden, col_start, slice_width, 1).astype(
        jnp.float32
    )
    gain_cols = lax.dynamic_slice_in_dim(student_gain, col_start, slice_width, 0)
    grad_gain = over_copies(jnp.sum(normed_grads * hidden_cols * inv_scale, axis=0), "branch")
    row_dots = over_copies(jnp.sum(gain_cols[None, :] * normed_grads * hidden_cols, axis=1), TOK)
    grad_hidden = (
        inv_scale * gain_cols[None, :] * normed_grads
        - hidden_cols * inv_scale**3 * row_dots[:, None] / width
    )
    exchanged = lax.all_to_all(student_normed, "branch", split_axis=1, concat_axis=0, tiled=True)
    all_grads = gathered_copies(logit_grads, "branch", 0)
    grad_head = lax.dot_general(
        exchanged, all_grads, (((0,), (0,)), ((), ())), preferred_element_type=jnp.float32
    )
    return (grad_head, grad_hidden, grad_gain)


def solution(mesh):
    split = Mesh(
        mesh.devices.reshape(mesh.shape["branch"], 4, 2, 4, 2),
        ("branch", "tok_0", "tok_1", "tok_2", "tok_3"),
    )
    in_specs = (
        P("branch", TOK, None),
        P("branch", None),
        P("branch", None, TOK),
        P("branch", None),
        P(),
        P("branch", TOK),
        P(None, "branch"),
        P("branch"),
    )
    out_specs = (P("branch", TOK), P("branch", TOK), P(TOK))
    return jax.shard_map(
        per_device, mesh=split, in_specs=in_specs, out_specs=out_specs, check_vma=False
    )
```

```python
import jax
import jax.numpy as jnp
from jax import lax
from jax.experimental import pallas as pl
from jax.experimental.pallas import tpu as pltpu
from jax.sharding import Mesh
from jax.sharding import PartitionSpec as P

DEN = 64
eps = 1e-05
mix_label = 0.25
loss_scale = 64.0
width_of_model = 4096
MESH = pl.DeviceIdType.MESH
B, Y, H, X, C = "branch", "tok_0", "tok_1", "tok_2", "tok_3"
TOK = (Y, H, X, C)


def ring(value, step, size):
    return lax.rem(value + (step + size), size)


def gather_kernel(
    block_ref, head_ref, piece_ref, out_ref, heads_ref, slices_ref,
    local_sem, send_sem, recv_sem, head_send, head_recv, piece_send, piece_recv,
):
    b = lax.axis_index(B)
    y, h, x, c = (lax.axis_index(name) for name in TOK)
    barrier = pltpu.get_barrier_semaphore()
    peers = [
        {X: ring(x, 1, 4)}, {X: ring(x, -1, 4)}, {Y: ring(y, 1, 4)}, {Y: ring(y, -1, 4)},
        {H: 1 - h}, {C: 1 - c},
    ] + [{B: ring(b, step, 8)} for step in range(1, 8)]
    for peer in peers:
        pl.semaphore_signal(barrier, inc=1, device_id=peer, device_id_type=MESH)
    pl.semaphore_wait(barrier, len(peers))

    numbers = iter(range(128))
    sent = []
    last = []

    def remote(source, target, send, recv, peer):
        return pltpu.make_async_remote_copy(
            src_ref=source, dst_ref=target, send_sem=send, recv_sem=recv,
            device_id=peer, device_id_type=MESH,
        )

    def move(piece, peer, arriving, source=None):
        number = next(numbers)
        send, recv = send_sem.at[number], recv_sem.at[number]
        copy = remote(piece if source is None else source, piece, send, recv, peer)
        copy.start()
        sent.append(copy)
        return remote(arriving, arriving, send, recv, peer).wait_recv

    def route(ref, side, plane, source):
        half = ref.shape[-1] // 2
        start = side * half
        cols = pl.ds(start, half)
        quarters = (pl.ds(start, half // 2), pl.ds(start + half // 2, half // 2))
        axis, other = ((X, Y), (Y, X))[side]
        mine, theirs = ((x, y), (y, x))[side]
        every = pl.ds(0, 4)

        def near(step, cs):
            at = ring(mine, step, 4)
            return ref.at[y, plane, at, c, :, cs] if side == 0 else ref.at[at, plane, x, c, :, cs]

        def rows(step, core, cs):
            at = ring(theirs, step, 4)
            return ref.at[at, plane, every, core, :, cs] if side == 0 else ref.at[every, plane, at, core, :, cs]

        def share(step):
            last.append(move(rows(step, c, cols), {C: 1 - c}, rows(step, 1 - c, cols)))

        forth, back = {axis: ring(mine, 1, 4)}, {axis: ring(mine, -1, 4)}
        first = None if source is None else source.at[:, cols]
        up = move(near(0, cols), forth, near(-1, cols), first)
        down = move(near(0, cols), back, near(1, cols), first)
        yield
        up()
        far_up = move(near(-1, quarters[0]), forth, near(2, quarters[0]))
        down()
        far_down = move(near(1, quarters[1]), back, near(2, quarters[1]))
        yield
        far_up()
        far_down()
        forth, back = {other: ring(theirs, 1, 4)}, {other: ring(theirs, -1, 4)}
        up = move(rows(0, c, cols), forth, rows(-1, c, cols))
        down = move(rows(0, c, cols), back, rows(1, c, cols))
        share(0)
        yield
        up()
        far_up = move(rows(-1, c, quarters[0]), forth, rows(2, c, quarters[0]))
        down()
        far_down = move(rows(1, c, quarters[1]), back, rows(2, c, quarters[1]))
        share(-1)
        share(1)
        yield
        far_up()
        far_down()
        share(2)

    def head_copies(step):
        up = remote(
            head_ref if step == 0 else heads_ref.at[jnp.maximum(b - step, 0)], heads_ref.at[jnp.maximum(b - step, 0)],
            head_send.at[0, step], head_recv.at[0, step], {B: jnp.minimum(b + 1, 7)},
        )
        down = remote(
            head_ref if step == 0 else heads_ref.at[jnp.minimum(b + step, 7)], heads_ref.at[jnp.minimum(b + step, 7)],
            head_send.at[1, step], head_recv.at[1, step], {B: jnp.maximum(b - 1, 0)},
        )
        return (
            (up, jnp.logical_and(b < 7, b >= step), b >= step + 1),
            (down, jnp.logical_and(b > 0, b + step <= 7), b + step <= 6),
        )

    def head_start(step):
        for copy, sends, _ in head_copies(step):
            pl.when(sends)(copy.start)

    def head_arrive(step):
        for copy, _, receives in head_copies(step):
            pl.when(receives)(copy.wait_recv)

    def head_sent(step):
        for copy, sends, _ in head_copies(step):
            pl.when(sends)(copy.wait_send)

    def head_next(step):
        head_arrive(step - 1)
        head_start(step)

    own = pltpu.make_async_copy(block_ref, out_ref.at[y, h, x, c], local_sem.at[0])
    own_head = pltpu.make_async_copy(head_ref, heads_ref.at[b], local_sem.at[1])
    across = move(out_ref.at[y, h, x, c], {H: 1 - h}, out_ref.at[y, 1 - h, x, c], block_ref)
    own.start()

    def piece_at(slot):
        return slices_ref.at[y, h, x, c, :, pl.ds(pl.multiple_of(128 * slot, 128), 128)]

    slot = lax.rem(b, 4)
    gives = (b // 4) == c
    pieces = [
        remote(
            piece_ref.at[ring(b, step, 8)], piece_at(slot), piece_send.at[step - 1], piece_recv.at[slot],
            {B: ring(b, step, 8)},
        )
        for step in range(1, 8)
    ]
    own_piece = pltpu.make_async_copy(piece_ref.at[b], piece_at(slot), local_sem.at[2])

    @pl.when(gives)
    def _():
        own_piece.start()
        for piece in pieces:
            piece.start()

    def pieces_arrive():
        for number in range(4):
            arriving = remote(
                piece_at(number), piece_at(number), piece_send.at[0], piece_recv.at[number], {B: ring(b, 1, 8)}
            )
            pl.when(b != 4 * c + number)(arriving.wait_recv)

        @pl.when(gives)
        def _():
            own_piece.wait()

    routes = [route(out_ref, 0, h, block_ref), route(out_ref, 1, h, block_ref)]
    late = [route(out_ref, 0, 1 - h, None), route(out_ref, 1, 1 - h, None)]
    thin = [route(slices_ref, 0, h, None), route(slices_ref, 1, h, None)]
    thin_late = [route(slices_ref, 0, 1 - h, None), route(slices_ref, 1, 1 - h, None)]

    def go(*groups):
        for group in groups:
            for r in group:
                next(r, None)

    go(routes)
    head_start(0)
    own_head.start()
    go(routes)
    pieces_arrive()
    thin_across = move(slices_ref.at[y, h, x, c], {H: 1 - h}, slices_ref.at[y, 1 - h, x, c])
    own.wait()
    go(routes, thin)
    head_next(1)
    go(routes, thin)
    across()
    go(late, routes, thin)
    head_next(2)
    thin_across()
    go(late, thin, thin_late)
    go(late, thin, thin_late)
    head_next(3)
    go(late, thin_late)
    head_next(4)
    go(late, thin_late)
    go(thin_late)
    head_next(5)
    head_next(6)
    head_arrive(6)
    own_head.wait()
    for arrive in last:
        arrive()
    for copy in sent:
        copy.wait_send()
    for step in range(7):
        head_sent(step)

    @pl.when(gives)
    def _():
        for piece in pieces:
            piece.wait_send()


def gather_all(block, head, pieces):
    rows, width = block.shape
    anywhere = pl.BlockSpec(memory_space=pl.ANY)
    return pl.pallas_call(
        gather_kernel,
        out_shape=(
            jax.ShapeDtypeStruct((4, 2, 4, 2, rows, width), block.dtype),
            jax.ShapeDtypeStruct((8, *head.shape), head.dtype),
            jax.ShapeDtypeStruct((4, 2, 4, 2, 16, 512), pieces.dtype),
        ),
        in_specs=[anywhere] * 3,
        out_specs=(anywhere,) * 3,
        scratch_shapes=[
            pltpu.SemaphoreType.DMA((3,)),
            pltpu.SemaphoreType.DMA((128,)),
            pltpu.SemaphoreType.DMA((128,)),
            pltpu.SemaphoreType.DMA((2, 7)),
            pltpu.SemaphoreType.DMA((2, 7)),
            pltpu.SemaphoreType.DMA((7,)),
            pltpu.SemaphoreType.DMA((4,)),
        ],
        compiler_params=pltpu.CompilerParams(collective_id=0, has_side_effects=True),
        name="gather_all",
    )(block, head, pieces)


def normalize(hidden, gain):
    values = hidden.astype(jnp.float32)
    inv_scale = lax.rsqrt(jnp.mean(values * values, axis=-1, keepdims=True) + eps)
    return ((values * inv_scale * gain).astype(jnp.bfloat16), inv_scale)


def finish_kernel(
    terms_ref, stats_ref, weight_ref, normed_ref, label_ref, heads_ref, hidden_ref, gain_ref,
    cols_ref, cols_gain_ref, inv_ref,
    grads_ref, hidden_out_ref, gain_out_ref,
    got_terms, near_stats, far_stats, factor, got_factor, grads, own_part, give_part, got_part,
    plane_give, plane_got, dots, dots_near, dots_far, piece, halves, sums, got_sums,
    local_sem, term_send, term_recv, near_send, near_recv, far_send, far_recv, factor_send, factor_recv,
    grad_send, grad_recv, part_send, part_recv, plane_send, plane_recv, dots_send, dots_recv,
    dot_near_send, dot_near_recv, half_send, half_recv, sum_send, sum_recv,
):
    b = lax.axis_index(B)
    y, h, x, c = (lax.axis_index(name) for name in TOK)
    along = [{B: ring(b, step, 8)} for step in range(1, 8)]
    near = [{H: h, C: 1 - c}, {H: 1 - h, C: c}, {H: 1 - h, C: 1 - c}]
    plane = [(dy, dx) for dy in range(4) for dx in range(4) if dy or dx]
    there = [{Y: ring(y, dy, 4), X: ring(x, dx, 4)} for dy, dx in plane]

    barrier = pltpu.get_barrier_semaphore()
    for peer in along + near + there:
        pl.semaphore_signal(barrier, inc=1, device_id=peer, device_id_type=MESH)
    pl.semaphore_wait(barrier, len(along) + len(near) + len(there))
    sent = []

    def move(source, target, send, recv, peer):
        copy = pltpu.make_async_remote_copy(
            src_ref=source, dst_ref=target, send_sem=send, recv_sem=recv, device_id=peer, device_id_type=MESH
        )
        copy.start()
        sent.append(copy)

    def arrive(target, send, recv, peer):
        pltpu.make_async_remote_copy(
            src_ref=target, dst_ref=target, send_sem=send, recv_sem=recv, device_id=peer, device_id_type=MESH
        ).wait_recv()

    def spread(source_of, target, send, recv):
        for n, peer in enumerate(along):
            move(source_of(peer[B]), target.at[b], send.at[n], recv.at[n], peer)

    def collect(target, send, recv):
        for n in range(7):
            arrive(target.at[ring(b, -(n + 1), 8)], send.at[n], recv.at[n], along[n])

    own_terms = pltpu.make_async_copy(terms_ref.at[b], got_terms.at[b], local_sem.at[0])
    own_terms.start()
    spread(lambda at: terms_ref.at[at], got_terms, term_send, term_recv)

    def add_block(q, total):
        columns = normed_ref[:, pl.ds(pl.multiple_of(q * 512, 512), 512)]
        return total + lax.dot_general(
            heads_ref[q], columns, (((1,), (1,)), ((), ())), preferred_element_type=jnp.float32
        )

    logits = lax.fori_loop(0, 8, add_block, jnp.zeros((320, 128), jnp.float32))
    local_top = jnp.max(logits, axis=0, keepdims=True)
    scaled = jnp.exp(logits - local_top)
    stats_ref_own = near_stats.at[0]
    stats_ref_own[...] = stats_ref[...]
    near_stats[0, 0, 8:9, :] = local_top
    near_stats[0, 1, 8:9, :] = jnp.sum(scaled, axis=0, keepdims=True)
    for n, peer in enumerate(near):
        move(near_stats.at[0], near_stats.at[n + 1], near_send.at[n], near_recv.at[n], peer)
    for n, peer in enumerate(near):
        arrive(near_stats.at[n + 1], near_send.at[n], near_recv.at[n], peer)

    def joined(stats, count):
        top = stats[0, 0]
        for n in range(1, count):
            top = jnp.maximum(top, stats[n, 0])
        total = jnp.zeros_like(top)
        for n in range(count):
            total += stats[n, 1] * jnp.exp(stats[n, 0] - top)
        return top, total

    top, total = joined(near_stats, 4)
    far_stats[0, 0] = top
    far_stats[0, 1] = total
    for n, peer in enumerate(there):
        move(far_stats.at[0], far_stats.at[n + 1], far_send.at[n], far_recv.at[n], peer)
    for n, peer in enumerate(there):
        arrive(far_stats.at[n + 1], far_send.at[n], far_recv.at[n], peer)
    top, total = joined(far_stats, 16)
    ratio = jnp.exp(near_stats[0, 0] - top) / total
    factor[...] = ratio[0:8] * weight_ref[...]
    own_ratio = ratio[8:9]
    got_factor[b] = factor[...]
    spread(lambda at: factor, got_factor, factor_send, factor_recv)
    collect(got_factor, factor_send, factor_recv)
    collect(got_terms, term_send, term_recv)
    own_terms.wait()

    def add_branch(n, mixed):
        return mixed + got_terms[n].astype(jnp.float32) * got_factor[n, pl.ds(b, 1), :]

    mixed = lax.fori_loop(0, 8, add_branch, jnp.zeros((320, 128), jnp.float32))
    targets = (1.0 - mix_label) * mixed + mix_label * label_ref[...]
    grads[...] = (loss_scale * (scaled * own_ratio - targets)).astype(jnp.bfloat16)
    own_grads = pltpu.make_async_copy(grads, grads_ref.at[b], local_sem.at[1])
    own_grads.start()
    spread(lambda at: grads, grads_ref, grad_send, grad_recv)

    def part(q):
        result = lax.dot_general(
            grads[...], heads_ref[q], (((0,), (0,)), ((), ())), preferred_element_type=jnp.float32
        )
        columns = pl.ds(pl.multiple_of(q * 512, 512), 512)
        weighted = hidden_ref[:, columns].astype(jnp.float32) * gain_ref[:, columns]
        return result, jnp.sum(result * weighted, axis=1, keepdims=True)

    column_dots = jnp.zeros((128, 1), jnp.float32)
    for n in range(4):
        result, dot = part(2 * n + (1 - c))
        give_part[n] = result
        column_dots += dot
        move(give_part.at[n], got_part.at[n], part_send.at[n], part_recv.at[n], {C: 1 - c})
    for n in range(4):
        result, dot = part(2 * n + c)
        own_part[n] = result
        column_dots += dot
    dots[0] = jnp.broadcast_to(column_dots, (128, 128)).T[0:8]
    for n, peer in enumerate(there):
        move(dots.at[0], dots_far.at[n], dots_send.at[n], dots_recv.at[n], peer)
    for n in range(4):
        arrive(got_part.at[n], part_send.at[n], part_recv.at[n], {C: 1 - c})
        both = own_part[n] + got_part[n]
        for m in range(4):
            plane_give[n, m] = both[:, 128 * m : 128 * m + 128].astype(jnp.bfloat16)
    for n, peer in enumerate(there):
        move(plane_give.at[peer[Y], peer[X]], plane_got.at[n], plane_send.at[n], plane_recv.at[n], peer)
    row_dots = dots[0]
    for n, peer in enumerate(there):
        arrive(dots_far.at[n], dots_send.at[n], dots_recv.at[n], peer)
        row_dots += dots_far[n]
    dots_near[0] = row_dots
    for n, peer in enumerate(near):
        move(dots_near.at[0], dots_near.at[n + 1], dot_near_send.at[n], dot_near_recv.at[n], peer)
    block = plane_give[y, x].astype(jnp.float32)
    for n, peer in enumerate(there):
        arrive(plane_got.at[n], plane_send.at[n], plane_recv.at[n], peer)
        block += plane_got[n].astype(jnp.float32)
    turned = block.T
    piece[0] = turned[0:64]
    piece[1] = turned[64:128]
    for core in range(2):
        mine = jnp.logical_and(h == c, c == core)
        copy = pltpu.make_async_remote_copy(
            src_ref=piece.at[core], dst_ref=halves.at[h], send_sem=half_send.at[core], recv_sem=half_recv.at[h],
            device_id={H: c, C: core}, device_id_type=MESH,
        )

        @pl.when(jnp.logical_not(mine))
        def _():
            copy.start()

        @pl.when(mine)
        def _():
            halves[h] = piece[core]

    for n, peer in enumerate(near):
        arrive(dots_near.at[n + 1], dot_near_send.at[n], dot_near_recv.at[n], peer)
    row_dot = (dots_near[0] + dots_near[1] + dots_near[2] + dots_near[3])[0:1]
    for source in range(2):
        waits = pltpu.make_async_remote_copy(
            src_ref=halves.at[source], dst_ref=halves.at[source], send_sem=half_send.at[0],
            recv_sem=half_recv.at[source], device_id={C: 1 - c}, device_id_type=MESH,
        )
        pl.when(jnp.logical_not(jnp.logical_and(h == source, c == h)))(waits.wait_recv)
    normed_grads = halves[0] + halves[1]
    inv_scale = inv_ref[...]
    values = cols_ref[...]
    terms = normed_grads * values * inv_scale
    sums[...] = jnp.broadcast_to(
        jnp.sum(jnp.concatenate([terms, terms], axis=0).T, axis=0, keepdims=True), (8, 128)
    )
    got_sums[b] = sums[...]
    spread(lambda at: sums, got_sums, sum_send, sum_recv)
    hidden_out_ref[...] = (
        inv_scale * cols_gain_ref[...] * normed_grads - values * inv_scale**3 * row_dot / width_of_model
    )
    collect(grads_ref, grad_send, grad_recv)
    own_grads.wait()
    collect(got_sums, sum_send, sum_recv)
    gain = got_sums[0]
    for n in range(1, 8):
        gain += got_sums[n]
    gain_out_ref[...] = gain
    for copy in sent:
        copy.wait_send()
    for core in range(2):
        mine = jnp.logical_and(h == c, c == core)
        copy = pltpu.make_async_remote_copy(
            src_ref=piece.at[core], dst_ref=halves.at[h], send_sem=half_send.at[core], recv_sem=half_recv.at[h],
            device_id={H: c, C: core}, device_id_type=MESH,
        )
        pl.when(jnp.logical_not(mine))(copy.wait_send)


def finish(*operands):
    inside = pl.BlockSpec(memory_space=pltpu.VMEM)
    anywhere = pl.BlockSpec(memory_space=pl.ANY)
    f32, bf16 = jnp.float32, jnp.bfloat16
    dma = pltpu.SemaphoreType.DMA
    pairs = [7, 3, 15, 7, 7, 4, 15, 15, 3, 2, 7]
    return pl.pallas_call(
        finish_kernel,
        out_shape=(
            jax.ShapeDtypeStruct((8, 320, 128), bf16),
            jax.ShapeDtypeStruct((64, 128), f32),
            jax.ShapeDtypeStruct((8, 128), f32),
        ),
        in_specs=[inside] * len(operands),
        out_specs=(anywhere, inside, inside),
        scratch_shapes=[
            pltpu.VMEM((8, 320, 128), bf16),
            pltpu.VMEM((4, 2, 16, 128), f32),
            pltpu.VMEM((16, 2, 16, 128), f32),
            pltpu.VMEM((8, 128), f32),
            pltpu.VMEM((8, 8, 128), f32),
            pltpu.VMEM((320, 128), bf16),
            pltpu.VMEM((4, 128, 512), f32),
            pltpu.VMEM((4, 128, 512), f32),
            pltpu.VMEM((4, 128, 512), f32),
            pltpu.VMEM((4, 4, 128, 128), bf16),
            pltpu.VMEM((15, 128, 128), bf16),
            pltpu.VMEM((1, 8, 128), f32),
            pltpu.VMEM((4, 8, 128), f32),
            pltpu.VMEM((15, 8, 128), f32),
            pltpu.VMEM((2, 64, 128), f32),
            pltpu.VMEM((2, 64, 128), f32),
            pltpu.VMEM((8, 128), f32),
            pltpu.VMEM((8, 8, 128), f32),
            dma((2,)),
        ] + [dma((n,)) for n in pairs for _ in range(2)],
        compiler_params=pltpu.CompilerParams(collective_id=1, has_side_effects=True, vmem_limit_bytes=48 << 20),
        name="finish",
    )(*operands)


def per_device(
    teacher_hidden, teacher_gain, teacher_head, student_hidden, student_gain, student_head, cluster_weights, token_ids
):
    cols = student_head.shape[1]
    place = lax.axis_index(TOK)
    own_normed, _ = normalize(teacher_hidden[0], teacher_gain[0])
    student_normed, inv_scale = normalize(student_hidden, student_gain)
    four = lax.dynamic_slice_in_dim(student_normed, 4 * (place // 2), 4, 0)
    pieces = four.reshape(4, 8, 512).transpose(1, 0, 2).reshape(8, 16, 128)
    normed, heads, slices = gather_all(own_normed, student_head.T, pieces)
    normed = normed.reshape(1024, 4096)
    logits = lax.dot_general(
        teacher_head[0].T, normed, (((1,), (1,)), ((), ())), preferred_element_type=jnp.float32
    )
    top = jnp.max(logits, axis=0)
    scaled = jnp.exp(logits - top)
    total = jnp.sum(scaled, axis=0)
    terms = scaled.astype(jnp.bfloat16).reshape(320, 8, 128).transpose(1, 0, 2)
    stats = jnp.pad(jnp.stack([top.reshape(8, 128), total.reshape(8, 128)]), ((0, 0), (0, 8), (0, 0)))
    weight = (cluster_weights[:, 0].astype(jnp.float32) / DEN).reshape(8, 128)
    offset = place * cols
    label = (token_ids[None, :] == offset + jnp.arange(cols, dtype=jnp.int32)[:, None]).astype(jnp.float32)
    hidden_cols = lax.dynamic_slice_in_dim(student_hidden, place * 64, 64, 1).astype(jnp.float32).T
    gain_cols = lax.dynamic_slice_in_dim(student_gain, place * 64, 64, 0)
    grads, grad_hidden, grad_gain = finish(
        terms, stats, weight, student_normed, label, heads, student_hidden, student_gain[None, :],
        hidden_cols, jnp.broadcast_to(gain_cols[:, None], (64, 128)), inv_scale.reshape(1, 128),
    )
    slices = slices.reshape(32, 2, 16, 4, 128).transpose(1, 3, 0, 2, 4).reshape(8, 128, 512)
    grad_head = lax.dot_general(
        grads, slices, (((0, 2), (0, 1)), ((), ())), preferred_element_type=jnp.float32
    )
    return (grad_head.T, grad_hidden.T, grad_gain[0, :64])


def solution(mesh):
    split = Mesh(mesh.devices.reshape(mesh.shape["branch"], 4, 2, 4, 2), (B, *TOK))
    in_specs = (
        P("branch", TOK, None), P("branch", None), P("branch", None, TOK), P("branch", None), P(),
        P("branch", TOK), P(None, "branch"), P("branch"),
    )
    out_specs = (P("branch", TOK), P("branch", TOK), P(TOK))
    return jax.shard_map(per_device, mesh=split, in_specs=in_specs, out_specs=out_specs, check_vma=False)
```

```python
import jax
import jax.numpy as jnp
from jax import lax
from jax.experimental import pallas as pl
from jax.experimental.pallas import tpu as pltpu
from jax.sharding import Mesh
from jax.sharding import PartitionSpec as P

DEN = 64
eps = 1e-05
mix_label = 0.25
loss_scale = 64.0
width_of_model = 4096
MESH = pl.DeviceIdType.MESH
B, Y, H, X, C = "branch", "tok_0", "tok_1", "tok_2", "tok_3"
TOK = (Y, H, X, C)


def ring(value, step, size):
    return lax.rem(value + (step + size), size)


def kernel(
    hidden_block_ref, teacher_gain_ref, teacher_head_ref, hidden_ref, gain_ref, head_ref,
    weight_ref, label_ref, cols_ref, cols_gain_ref,
    grad_head_ref, hidden_out_ref, gain_out_ref,
    states, head_cols, heads, normed, slices, joined_slices, inv_cols,
    terms, got_terms, near_stats, far_stats, near_student, far_student, factor, got_factor, all_grads,
    own_part, give_part, got_part, plane_give, plane_got, dots, dots_near, dots_far, piece, halves, sums, got_sums,
    local_sem, send_sem, recv_sem, head_send, head_recv, piece_send, piece_recv,
    term_send, term_recv, near_send, near_recv, far_send, far_recv,
    student_near_send, student_near_recv, student_far_send, student_far_recv, factor_send, factor_recv,
    grad_send, grad_recv, part_send, part_recv, plane_send, plane_recv, dots_send, dots_recv,
    dot_near_send, dot_near_recv, half_send, half_recv, sum_send, sum_recv,
):
    b = lax.axis_index(B)
    y, h, x, c = (lax.axis_index(name) for name in TOK)
    along = [{B: ring(b, step, 8)} for step in range(1, 8)]
    near = [{H: h, C: 1 - c}, {H: 1 - h, C: c}, {H: 1 - h, C: 1 - c}]
    plane = [(dy, dx) for dy in range(4) for dx in range(4) if dy or dx]
    there = [{Y: ring(y, dy, 4), X: ring(x, dx, 4)} for dy, dx in plane]

    barrier = pltpu.get_barrier_semaphore()
    for peer in near + along + there:
        pl.semaphore_signal(barrier, inc=1, device_id=peer, device_id_type=MESH)
    own_teacher_head = pltpu.make_async_copy(teacher_head_ref, head_cols, local_sem.at[0])
    own_teacher_head.start()
    own_head = pltpu.make_async_copy(head_ref, heads.at[b], local_sem.at[1])
    own_head.start()

    def unit_rows(hidden, gain):
        values = hidden.astype(jnp.float32)
        inv_scale = lax.rsqrt(jnp.mean(values * values, axis=-1, keepdims=True) + eps)
        return (values * inv_scale * gain).astype(jnp.bfloat16), inv_scale

    states[y, h, x, c] = unit_rows(hidden_block_ref[...], teacher_gain_ref[...])[0]
    pl.semaphore_wait(barrier, len(near) + len(along) + len(there))

    numbers = iter(range(128))
    sent = []

    def remote(source, target, send, recv, peer):
        return pltpu.make_async_remote_copy(
            src_ref=source, dst_ref=target, send_sem=send, recv_sem=recv, device_id=peer, device_id_type=MESH
        )

    def move(source, target, send, recv, peer):
        copy = remote(source, target, send, recv, peer)
        copy.start()
        sent.append(copy)

    def arrive(target, send, recv, peer):
        remote(target, target, send, recv, peer).wait_recv()

    def step_of(part, peer, arriving):
        number = next(numbers)
        send, recv = send_sem.at[number], recv_sem.at[number]
        move(part, part, send, recv, peer)
        return remote(arriving, arriving, send, recv, peer).wait_recv

    def spread(source_of, target, send, recv):
        for n, peer in enumerate(along):
            move(source_of(peer[B]), target.at[b], send.at[n], recv.at[n], peer)

    def collect(target, send, recv):
        for n in range(7):
            arrive(target.at[ring(b, -(n + 1), 8)], send.at[n], recv.at[n], along[n])

    def route(ref, side, layer, shared):
        half = ref.shape[-1] // 2
        start = side * half
        cols = pl.ds(start, half)
        quarters = (pl.ds(start, half // 2), pl.ds(start + half // 2, half // 2))
        axis, other = ((X, Y), (Y, X))[side]
        mine, theirs = ((x, y), (y, x))[side]
        every = pl.ds(0, 4)

        def beside(step, cs):
            at = ring(mine, step, 4)
            return ref.at[y, layer, at, c, :, cs] if side == 0 else ref.at[at, layer, x, c, :, cs]

        def rows(step, core, cs):
            at = ring(theirs, step, 4)
            return ref.at[at, layer, every, core, :, cs] if side == 0 else ref.at[every, layer, at, core, :, cs]

        def share(step):
            shared.append(step_of(rows(step, c, cols), {C: 1 - c}, rows(step, 1 - c, cols)))

        forth, back = {axis: ring(mine, 1, 4)}, {axis: ring(mine, -1, 4)}
        up = step_of(beside(0, cols), forth, beside(-1, cols))
        down = step_of(beside(0, cols), back, beside(1, cols))
        yield
        up()
        far_up = step_of(beside(-1, quarters[0]), forth, beside(2, quarters[0]))
        down()
        far_down = step_of(beside(1, quarters[1]), back, beside(2, quarters[1]))
        yield
        far_up()
        far_down()
        forth, back = {other: ring(theirs, 1, 4)}, {other: ring(theirs, -1, 4)}
        up = step_of(rows(0, c, cols), forth, rows(-1, c, cols))
        down = step_of(rows(0, c, cols), back, rows(1, c, cols))
        share(0)
        yield
        up()
        far_up = step_of(rows(-1, c, quarters[0]), forth, rows(2, c, quarters[0]))
        down()
        far_down = step_of(rows(1, c, quarters[1]), back, rows(2, c, quarters[1]))
        share(-1)
        share(1)
        yield
        far_up()
        far_down()
        share(2)

    def head_copies(step, part):
        rows = pl.ds(160 * part, 160)
        low, high = jnp.maximum(b - step, 0), jnp.minimum(b + step, 7)
        up = remote(
            (head_ref if step == 0 else heads.at[low]).at[rows], heads.at[low, rows],
            head_send.at[0, step, part], head_recv.at[0, step, part], {B: jnp.minimum(b + 1, 7)},
        )
        down = remote(
            (head_ref if step == 0 else heads.at[high]).at[rows], heads.at[high, rows],
            head_send.at[1, step, part], head_recv.at[1, step, part], {B: jnp.maximum(b - 1, 0)},
        )
        return (
            (up, jnp.logical_and(b < 7, b >= step), b >= step + 1),
            (down, jnp.logical_and(b > 0, b + step <= 7), b + step <= 6),
        )

    def head_start(step, part):
        for copy, sends, _ in head_copies(step, part):
            pl.when(sends)(copy.start)

    def head_arrive(step, part):
        for copy, _, receives in head_copies(step, part):
            pl.when(receives)(copy.wait_recv)

    def head_sent(step, part):
        for copy, sends, _ in head_copies(step, part):
            pl.when(sends)(copy.wait_send)

    def head_next(step):
        for part in range(2):
            head_arrive(step - 1, part)
            head_start(step, part)

    slot = lax.rem(b, 4)
    gives = (b // 4) == c
    part_rows = pl.ds(pl.multiple_of(16 * (2 * y + h), 16), 16)

    def slice_part(at):
        return normed.at[part_rows, pl.ds(pl.multiple_of(512 * at + 128 * x, 128), 128)]

    def slice_at(number):
        return slices.at[y, h, x, c, :, pl.ds(pl.multiple_of(128 * number, 128), 128)]

    slice_copies = [
        remote(slice_part(peer[B]), slice_at(slot), piece_send.at[n], piece_recv.at[slot], peer)
        for n, peer in enumerate(along)
    ]
    own_slice = pltpu.make_async_copy(slice_part(b), slice_at(slot), local_sem.at[2])

    def slices_start():
        @pl.when(gives)
        def _():
            own_slice.start()
            for copy in slice_copies:
                copy.start()

    def slices_arrive():
        for number in range(4):
            arriving = remote(slice_at(number), slice_at(number), piece_send.at[0], piece_recv.at[number], along[0])
            pl.when(b != 4 * c + number)(arriving.wait_recv)
        pl.when(gives)(own_slice.wait)

    def norm_student(n, carry):
        rows = pl.ds(pl.multiple_of(16 * n, 16), 16)
        unit, inv_scale = unit_rows(hidden_ref[rows, :], gain_ref[...])
        normed[rows, :] = unit
        inv_cols[rows, :] = jnp.broadcast_to(inv_scale, (16, 128))
        return carry

    def term_copy(row, layer):
        to = 2 * row + layer
        return to, remote(terms.at[to], got_terms.at[b], term_send.at[to], term_recv.at[b], {B: to})

    def teach(row, layer):
        to, copy = term_copy(row, layer)

        def add_columns(k, total):
            columns = pl.ds(pl.multiple_of(1024 * k, 1024), 1024)
            return total + lax.dot_general(
                head_cols[:, columns], states[row, layer, :, :, :, columns].reshape(128, 1024),
                (((1,), (1,)), ((), ())), preferred_element_type=jnp.float32,
            )

        logits = lax.fori_loop(0, 4, add_columns, jnp.zeros((320, 128), jnp.float32))
        top = jnp.max(logits, axis=0, keepdims=True)
        scaled = jnp.exp(logits - top)
        near_stats[0, 0, pl.ds(to, 1), :] = top
        near_stats[0, 1, pl.ds(to, 1), :] = jnp.sum(scaled, axis=0, keepdims=True)
        terms[to] = scaled.astype(jnp.bfloat16)
        pl.when(to != b)(copy.start)

        @pl.when(to == b)
        def _():
            got_terms[b] = terms[to]

    def joined(stats, count):
        top = stats[0, 0]
        for n in range(1, count):
            top = jnp.maximum(top, stats[n, 0])
        total = jnp.zeros_like(top)
        for n in range(count):
            total += stats[n, 1] * jnp.exp(stats[n, 0] - top)
        return top, total

    def to_all(peers, stats, send, recv):
        for n, peer in enumerate(peers):
            move(stats.at[0], stats.at[n + 1], send.at[n], recv.at[n], peer)

    def from_all(peers, stats, send, recv):
        for n, peer in enumerate(peers):
            arrive(stats.at[n + 1], send.at[n], recv.at[n], peer)

    def near_to_far(close, far, send, recv, far_send, far_recv):
        from_all(near, close, send, recv)
        top, total = joined(close, 4)
        far[0, 0] = top
        far[0, 1] = total
        to_all(there, far, far_send, far_recv)

    def ratio_of(close, far, far_send, far_recv):
        from_all(there, far, far_send, far_recv)
        top, total = joined(far, 16)
        return jnp.exp(close[0, 0] - top) / total

    first_shared, late_shared, thin_shared = [], [], []
    first = [route(states, side, h, first_shared) for side in range(2)]
    late = [route(states, side, 1 - h, late_shared) for side in range(2)]
    thin = [route(slices, side, h, thin_shared) for side in range(2)]
    thin_late = [route(slices, side, 1 - h, thin_shared) for side in range(2)]

    def go(*groups):
        for group in groups:
            for r in group:
                next(r, None)

    across = step_of(states.at[y, h, x, c], {H: 1 - h}, states.at[y, 1 - h, x, c])
    go(first)
    lax.fori_loop(0, 8, norm_student, 0)
    slices_start()
    for part in range(2):
        head_start(0, part)
    go(first)
    slices_arrive()
    thin_across = step_of(slices.at[y, h, x, c], {H: 1 - h}, slices.at[y, 1 - h, x, c])
    go(first, thin)
    head_next(1)
    go(first, thin)
    across()
    go(late, first, thin)
    head_next(2)
    own_teacher_head.wait()
    for wait in first_shared:
        wait()
    go(late)
    teach(0, h)
    teach(1, h)
    go(late)
    teach(2, h)
    teach(3, h)
    thin_across()
    go(late, thin, thin_late)
    head_next(3)
    go(late, thin, thin_late)
    for wait in late_shared:
        wait()
    for row in range(4):
        teach(row, 1 - h)
    to_all(near, near_stats, near_send, near_recv)
    go(thin_late)
    head_next(4)
    near_to_far(near_stats, far_stats, near_send, near_recv, far_send, far_recv)
    go(thin_late)
    head_next(5)
    factor[...] = ratio_of(near_stats, far_stats, far_send, far_recv) * weight_ref[...]
    got_factor[b] = factor[...]
    spread(lambda at: factor, got_factor, factor_send, factor_recv)
    go(thin_late)
    head_next(6)
    for part in range(2):
        head_arrive(6, part)
    own_head.wait()

    def add_block(q, total):
        columns = normed[:, pl.ds(pl.multiple_of(q * 512, 512), 512)]
        return total + lax.dot_general(
            heads[q], columns, (((1,), (1,)), ((), ())), preferred_element_type=jnp.float32
        )

    logits = lax.fori_loop(0, 8, add_block, jnp.zeros((320, 128), jnp.float32))
    local_top = jnp.max(logits, axis=0, keepdims=True)
    scaled = jnp.exp(logits - local_top)
    near_student[0, 0] = jnp.broadcast_to(local_top, (8, 128))
    near_student[0, 1] = jnp.broadcast_to(jnp.sum(scaled, axis=0, keepdims=True), (8, 128))
    to_all(near, near_student, student_near_send, student_near_recv)
    near_to_far(near_student, far_student, student_near_send, student_near_recv, student_far_send, student_far_recv)
    for wait in thin_shared:
        wait()
    for at in range(8):
        for n in range(4):
            joined_slices[at, :, 128 * n : 128 * n + 128] = slices[
                :, :, n, at // 4, :, 128 * (at % 4) : 128 * (at % 4) + 128
            ].reshape(128, 128)
    own_ratio = ratio_of(near_student, far_student, student_far_send, student_far_recv)[0:1]
    collect(got_factor, factor_send, factor_recv)
    for n in range(8):
        waits = remote(got_terms.at[n], got_terms.at[n], term_send.at[n], term_recv.at[n], along[0])
        pl.when(b != n)(waits.wait_recv)

    def add_branch(n, mixed):
        return mixed + got_terms[n].astype(jnp.float32) * got_factor[n, pl.ds(b, 1), :]

    mixed = lax.fori_loop(0, 8, add_branch, jnp.zeros((320, 128), jnp.float32))
    targets = (1.0 - mix_label) * mixed + mix_label * label_ref[...]
    all_grads[b] = (loss_scale * (scaled * own_ratio - targets)).astype(jnp.bfloat16)

    low = 4 * (b // 4)
    mates = [low + ring(slot, step, 4) for step in range(1, 4)]
    sources = [low + ring(slot, -step, 4) for step in range(1, 4)]
    partner = ring(b, 4, 8)
    move(all_grads.at[b], all_grads.at[b], grad_send.at[3], grad_recv.at[3], {B: partner})
    for n, mate in enumerate(mates):
        move(all_grads.at[b], all_grads.at[b], grad_send.at[n], grad_recv.at[n], {B: mate})

    def part(q):
        result = lax.dot_general(
            all_grads[b], heads[q], (((0,), (0,)), ((), ())), preferred_element_type=jnp.float32
        )
        columns = pl.ds(pl.multiple_of(q * 512, 512), 512)
        weighted = hidden_ref[:, columns].astype(jnp.float32) * gain_ref[:, columns]
        return result, jnp.sum(result * weighted, axis=1, keepdims=True)

    column_dots = jnp.zeros((128, 1), jnp.float32)
    for n in range(4):
        result, dot = part(2 * n + (1 - c))
        give_part[n] = result
        column_dots += dot
        move(give_part.at[n], got_part.at[n], part_send.at[n], part_recv.at[n], {C: 1 - c})
    for n in range(4):
        result, dot = part(2 * n + c)
        own_part[n] = result
        column_dots += dot
    dots[0] = jnp.broadcast_to(column_dots, (128, 128)).T[0:8]
    for n, peer in enumerate(there):
        move(dots.at[0], dots_far.at[n], dots_send.at[n], dots_recv.at[n], peer)
    for n in range(4):
        arrive(got_part.at[n], part_send.at[n], part_recv.at[n], {C: 1 - c})
        both = own_part[n] + got_part[n]
        for m in range(4):
            plane_give[n, m] = both[:, 128 * m : 128 * m + 128].astype(jnp.bfloat16)
    for n, peer in enumerate(there):
        move(plane_give.at[peer[Y], peer[X]], plane_got.at[n], plane_send.at[n], plane_recv.at[n], peer)

    def pass_on():
        arrive(all_grads.at[partner], grad_send.at[3], grad_recv.at[3], {B: partner})
        for n, mate in enumerate(mates):
            move(all_grads.at[partner], all_grads.at[partner], grad_send.at[4 + n], grad_recv.at[4 + n], {B: mate})

    def add_head(at):
        grad_head_ref[...] += jnp.dot(all_grads[at], joined_slices[at], preferred_element_type=jnp.float32)

    row_dots = dots[0]
    for n, peer in enumerate(there):
        arrive(dots_far.at[n], dots_send.at[n], dots_recv.at[n], peer)
        row_dots += dots_far[n]
    dots_near[0] = row_dots
    to_all(near, dots_near, dot_near_send, dot_near_recv)
    pass_on()
    block = plane_give[y, x].astype(jnp.float32)
    for n, peer in enumerate(there):
        arrive(plane_got.at[n], plane_send.at[n], plane_recv.at[n], peer)
        block += plane_got[n].astype(jnp.float32)
    turned = block.T
    piece[0] = turned[0:64]
    piece[1] = turned[64:128]
    half_copies = [
        remote(piece.at[core], halves.at[h], half_send.at[core], half_recv.at[h], {H: c, C: core}) for core in range(2)
    ]
    for core, copy in enumerate(half_copies):
        mine = jnp.logical_and(h == c, c == core)
        pl.when(jnp.logical_not(mine))(copy.start)

        @pl.when(mine)
        def _():
            halves[h] = piece[core]

    grad_head_ref[...] = jnp.dot(all_grads[b], joined_slices[b], preferred_element_type=jnp.float32)
    add_head(partner)
    from_all(near, dots_near, dot_near_send, dot_near_recv)
    row_dot = (dots_near[0] + dots_near[1] + dots_near[2] + dots_near[3])[0:1]
    for source in range(2):
        waits = remote(
            halves.at[source], halves.at[source], half_send.at[0], half_recv.at[source], {C: 1 - c}
        )
        pl.when(jnp.logical_not(jnp.logical_and(h == source, c == h)))(waits.wait_recv)
    normed_grads = halves[0] + halves[1]
    inv_scale = inv_cols[...].T[0:1]
    values = cols_ref[...]
    summands = normed_grads * values * inv_scale
    sums[...] = jnp.broadcast_to(
        jnp.sum(jnp.concatenate([summands, summands], axis=0).T, axis=0, keepdims=True), (8, 128)
    )
    got_sums[b] = sums[...]
    spread(lambda at: sums, got_sums, sum_send, sum_recv)
    hidden_out_ref[...] = (
        inv_scale * cols_gain_ref[...] * normed_grads - values * inv_scale**3 * row_dot / width_of_model
    )
    for n, source in enumerate(sources):
        arrive(all_grads.at[source], grad_send.at[n], grad_recv.at[n], {B: partner})
        add_head(source)
    for n, source in enumerate(sources):
        other = ring(source, 4, 8)
        arrive(all_grads.at[other], grad_send.at[4 + n], grad_recv.at[4 + n], {B: partner})
        add_head(other)
    collect(got_sums, sum_send, sum_recv)
    gain = got_sums[0]
    for n in range(1, 8):
        gain += got_sums[n]
    gain_out_ref[...] = gain

    for copy in sent:
        copy.wait_send()
    for step in range(7):
        for part_number in range(2):
            head_sent(step, part_number)

    @pl.when(gives)
    def _():
        for copy in slice_copies:
            copy.wait_send()

    for n in range(8):
        _, copy = term_copy(n // 2, n % 2)
        pl.when(b != n)(copy.wait_send)
    for core, copy in enumerate(half_copies):
        pl.when(jnp.logical_not(jnp.logical_and(h == c, c == core)))(copy.wait_send)


def run(*operands):
    inside = pl.BlockSpec(memory_space=pltpu.VMEM)
    anywhere = pl.BlockSpec(memory_space=pl.ANY)
    f32, bf16 = jnp.float32, jnp.bfloat16
    dma = pltpu.SemaphoreType.DMA
    arrays = [
        ((4, 2, 4, 2, 16, 4096), bf16), ((320, 4096), bf16), ((8, 320, 512), bf16), ((128, 4096), bf16),
        ((4, 2, 4, 2, 16, 512), bf16), ((8, 128, 512), bf16), ((128, 128), f32),
        ((8, 320, 128), bf16), ((8, 320, 128), bf16), ((4, 2, 8, 128), f32), ((16, 2, 8, 128), f32),
        ((4, 2, 8, 128), f32), ((16, 2, 8, 128), f32), ((8, 128), f32), ((8, 8, 128), f32), ((8, 320, 128), bf16),
        ((4, 128, 512), f32), ((4, 128, 512), f32), ((4, 128, 512), f32), ((4, 4, 128, 128), bf16),
        ((15, 128, 128), bf16), ((1, 8, 128), f32), ((4, 8, 128), f32), ((15, 8, 128), f32),
        ((2, 64, 128), f32), ((2, 64, 128), f32), ((8, 128), f32), ((8, 8, 128), f32),
    ]
    counts = [(128,), (2, 7, 2), None, (8,), (3,), (15,), (3,), (15,), (7,), (7,), (4,), (15,), (15,), (3,), (2,), (7,)]
    semaphores = [dma((3,))]
    for count in counts:
        semaphores += [dma((7,)), dma((4,))] if count is None else [dma(count), dma(count)]
    return pl.pallas_call(
        kernel,
        out_shape=(
            jax.ShapeDtypeStruct((320, 512), f32),
            jax.ShapeDtypeStruct((64, 128), f32),
            jax.ShapeDtypeStruct((8, 128), f32),
        ),
        in_specs=[inside, inside, anywhere, inside, inside, anywhere, inside, inside, inside, inside],
        out_specs=(inside,) * 3,
        scratch_shapes=[pltpu.VMEM(*array) for array in arrays] + semaphores,
        compiler_params=pltpu.CompilerParams(collective_id=0, has_side_effects=True, vmem_limit_bytes=56 << 20),
        name="distill",
    )(*operands)


def per_device(
    teacher_hidden, teacher_gain, teacher_head, student_hidden, student_gain, student_head, cluster_weights, token_ids
):
    cols = student_head.shape[1]
    place = lax.axis_index(TOK)
    weight = (cluster_weights[:, 0].astype(jnp.float32) / DEN).reshape(8, 128)
    offset = place * cols
    label = (token_ids[None, :] == offset + jnp.arange(cols, dtype=jnp.int32)[:, None]).astype(jnp.float32)
    hidden_cols = lax.dynamic_slice_in_dim(student_hidden, place * 64, 64, 1).astype(jnp.float32).T
    gain_cols = lax.dynamic_slice_in_dim(student_gain, place * 64, 64, 0)
    grad_head, grad_hidden, grad_gain = run(
        teacher_hidden[0], teacher_gain, teacher_head[0].T, student_hidden, student_gain[None, :], student_head.T,
        weight, label, hidden_cols, jnp.broadcast_to(gain_cols[:, None], (64, 128)),
    )
    return (grad_head.T, grad_hidden.T, grad_gain[0, :64])


def solution(mesh):
    split = Mesh(mesh.devices.reshape(mesh.shape["branch"], 4, 2, 4, 2), (B, *TOK))
    in_specs = (
        P("branch", TOK, None), P("branch", None), P("branch", None, TOK), P("branch", None), P(),
        P("branch", TOK), P(None, "branch"), P("branch"),
    )
    out_specs = (P("branch", TOK), P("branch", TOK), P(TOK))
    return jax.shard_map(per_device, mesh=split, in_specs=in_specs, out_specs=out_specs, check_vma=False)
```

```python
import jax
import jax.numpy as jnp
from jax import lax
from jax.experimental import pallas as pl
from jax.experimental.pallas import tpu as pltpu
from jax.sharding import Mesh
from jax.sharding import PartitionSpec as P

DEN = 64
eps = 1e-05
mix_label = 0.25
loss_scale = 64.0
width_of_model = 4096
MESH = pl.DeviceIdType.MESH
B, Y, H, X, C = "branch", "tok_0", "tok_1", "tok_2", "tok_3"
TOK = (Y, H, X, C)


def ring(value, step, size):
    return lax.rem(value + (step + size), size)


def kernel(
    hidden_block_ref, teacher_gain_ref, teacher_head_ref, hidden_ref, gain_ref, head_ref,
    weight_ref, label_ref,
    grad_head_ref, hidden_out_ref, gain_out_ref,
    states, head_cols, heads, normed, slices, joined_slices, inv_cols,
    terms, got_terms, near_stats, far_stats, near_student, far_student, factor, got_factor, all_grads,
    own_part, give_part, got_part, plane_give, plane_got, dots, dots_near, dots_far, piece, halves, sums, got_sums, chip,
    local_sem, send_sem, recv_sem, head_send, head_recv, piece_send, piece_recv,
    term_send, term_recv, near_send, near_recv, far_send, far_recv,
    student_near_send, student_near_recv, student_far_send, student_far_recv, factor_send, factor_recv,
    grad_send, grad_recv, part_send, part_recv, plane_send, plane_recv, dots_send, dots_recv,
    dot_near_send, dot_near_recv, half_send, half_recv, sum_send, sum_recv,
):
    b = lax.axis_index(B)
    y, h, x, c = (lax.axis_index(name) for name in TOK)
    along = [{B: ring(b, step, 8)} for step in range(1, 8)]
    near = [{H: h, C: 1 - c}, {H: 1 - h, C: c}, {H: 1 - h, C: 1 - c}]
    plane = [(dy, dx) for dy in range(4) for dx in range(4) if dy or dx]
    there = [{Y: ring(y, dy, 4), X: ring(x, dx, 4)} for dy, dx in plane]

    barrier = pltpu.get_barrier_semaphore()
    column = [
        {B: ring(b, step, 8), H: ring(h, dh, 2), C: ring(c, dc, 2)}
        for step in range(8) for dh in range(2) for dc in range(2) if step or dh or dc
    ]
    for peer in column + there:
        pl.semaphore_signal(barrier, inc=1, device_id=peer, device_id_type=MESH)
    own_teacher_head = pltpu.make_async_copy(teacher_head_ref, head_cols, local_sem.at[0])
    own_teacher_head.start()
    own_head = pltpu.make_async_copy(head_ref, heads.at[b], local_sem.at[1])
    own_head.start()

    def unit_rows(hidden, gain):
        values = hidden.astype(jnp.float32)
        inv_scale = lax.rsqrt(jnp.mean(values * values, axis=-1, keepdims=True) + eps)
        return (values * inv_scale * gain).astype(jnp.bfloat16), inv_scale

    states[y, h, x, c] = unit_rows(hidden_block_ref[...], teacher_gain_ref[...])[0]
    pl.semaphore_wait(barrier, len(column) + len(there))

    numbers = iter(range(128))
    sent = []

    def remote(source, target, send, recv, peer):
        return pltpu.make_async_remote_copy(
            src_ref=source, dst_ref=target, send_sem=send, recv_sem=recv, device_id=peer, device_id_type=MESH
        )

    def move(source, target, send, recv, peer):
        copy = remote(source, target, send, recv, peer)
        copy.start()
        sent.append(copy)

    def arrive(target, send, recv, peer):
        remote(target, target, send, recv, peer).wait_recv()

    def step_of(part, peer, arriving):
        number = next(numbers)
        send, recv = send_sem.at[number], recv_sem.at[number]
        move(part, part, send, recv, peer)
        return remote(arriving, arriving, send, recv, peer).wait_recv

    def spread(source_of, target, send, recv):
        for n, peer in enumerate(along):
            move(source_of(peer[B]), target.at[b], send.at[n], recv.at[n], peer)

    def collect(target, send, recv):
        for n in range(7):
            arrive(target.at[ring(b, -(n + 1), 8)], send.at[n], recv.at[n], along[n])

    def route(ref, side, layer, shared):
        half = ref.shape[-1] // 2
        start = side * half
        cols = pl.ds(start, half)
        quarters = (pl.ds(start, half // 2), pl.ds(start + half // 2, half // 2))
        axis, other = ((X, Y), (Y, X))[side]
        mine, theirs = ((x, y), (y, x))[side]
        every = pl.ds(0, 4)

        def beside(step, cs):
            at = ring(mine, step, 4)
            return ref.at[y, layer, at, c, :, cs] if side == 0 else ref.at[at, layer, x, c, :, cs]

        def rows(step, core, cs):
            at = ring(theirs, step, 4)
            return ref.at[at, layer, every, core, :, cs] if side == 0 else ref.at[every, layer, at, core, :, cs]

        def share(step):
            shared.append(step_of(rows(step, c, cols), {C: 1 - c}, rows(step, 1 - c, cols)))

        forth, back = {axis: ring(mine, 1, 4)}, {axis: ring(mine, -1, 4)}
        up = step_of(beside(0, cols), forth, beside(-1, cols))
        down = step_of(beside(0, cols), back, beside(1, cols))
        yield
        up()
        far_up = step_of(beside(-1, quarters[0]), forth, beside(2, quarters[0]))
        down()
        far_down = step_of(beside(1, quarters[1]), back, beside(2, quarters[1]))
        yield
        far_up()
        far_down()
        forth, back = {other: ring(theirs, 1, 4)}, {other: ring(theirs, -1, 4)}
        up = step_of(rows(0, c, cols), forth, rows(-1, c, cols))
        down = step_of(rows(0, c, cols), back, rows(1, c, cols))
        share(0)
        yield
        up()
        far_up = step_of(rows(-1, c, quarters[0]), forth, rows(2, c, quarters[0]))
        down()
        far_down = step_of(rows(1, c, quarters[1]), back, rows(2, c, quarters[1]))
        share(-1)
        share(1)
        yield
        far_up()
        far_down()
        share(2)

    def head_copies(step, part):
        rows = pl.ds(160 * part, 160)
        low, high = jnp.maximum(b - step, 0), jnp.minimum(b + step, 7)
        up = remote(
            (head_ref if step == 0 else heads.at[low]).at[rows], heads.at[low, rows],
            head_send.at[0, step, part], head_recv.at[0, step, part], {B: jnp.minimum(b + 1, 7)},
        )
        down = remote(
            (head_ref if step == 0 else heads.at[high]).at[rows], heads.at[high, rows],
            head_send.at[1, step, part], head_recv.at[1, step, part], {B: jnp.maximum(b - 1, 0)},
        )
        return (
            (up, jnp.logical_and(b < 7, b >= step), b >= step + 1),
            (down, jnp.logical_and(b > 0, b + step <= 7), b + step <= 6),
        )

    def head_start(step, part):
        for copy, sends, _ in head_copies(step, part):
            pl.when(sends)(copy.start)

    def head_arrive(step, part):
        for copy, _, receives in head_copies(step, part):
            pl.when(receives)(copy.wait_recv)

    def head_sent(step, part):
        for copy, sends, _ in head_copies(step, part):
            pl.when(sends)(copy.wait_send)

    def head_next(step):
        for part in range(2):
            head_arrive(step - 1, part)
            head_start(step, part)

    slot = lax.rem(b, 4)
    gives = (b // 4) == c
    part_rows = pl.ds(pl.multiple_of(16 * (2 * y + h), 16), 16)

    def slice_part(at):
        return normed.at[part_rows, pl.ds(pl.multiple_of(512 * at + 128 * x, 128), 128)]

    def slice_at(number):
        return slices.at[y, h, x, c, :, pl.ds(pl.multiple_of(128 * number, 128), 128)]

    slice_copies = [
        remote(slice_part(peer[B]), slice_at(slot), piece_send.at[n], piece_recv.at[slot], peer)
        for n, peer in enumerate(along)
    ]
    own_slice = pltpu.make_async_copy(slice_part(b), slice_at(slot), local_sem.at[2])

    def slices_start():
        @pl.when(gives)
        def _():
            own_slice.start()
            for copy in slice_copies:
                copy.start()

    def slices_arrive():
        for number in range(4):
            arriving = remote(slice_at(number), slice_at(number), piece_send.at[0], piece_recv.at[number], along[0])
            pl.when(b != 4 * c + number)(arriving.wait_recv)
        pl.when(gives)(own_slice.wait)

    def norm_student(n, carry):
        rows = pl.ds(pl.multiple_of(16 * n, 16), 16)
        unit, inv_scale = unit_rows(hidden_ref[rows, :], gain_ref[...])
        normed[rows, :] = unit
        inv_cols[rows, :] = jnp.broadcast_to(inv_scale, (16, 128))
        return carry

    def term_copy(row, layer):
        to = 2 * row + layer
        return to, remote(terms.at[to], got_terms.at[b], term_send.at[to], term_recv.at[b], {B: to})

    def teach(row, layer):
        to, copy = term_copy(row, layer)

        def add_columns(k, total):
            columns = pl.ds(pl.multiple_of(1024 * k, 1024), 1024)
            return total + lax.dot_general(
                head_cols[:, columns], states[row, layer, :, :, :, columns].reshape(128, 1024),
                (((1,), (1,)), ((), ())), preferred_element_type=jnp.float32,
            )

        logits = lax.fori_loop(0, 4, add_columns, jnp.zeros((320, 128), jnp.float32))
        top = jnp.max(logits, axis=0, keepdims=True)
        scaled = jnp.exp(logits - top)
        near_stats[0, 0, pl.ds(to, 1), :] = top
        near_stats[0, 1, pl.ds(to, 1), :] = jnp.sum(scaled, axis=0, keepdims=True)
        terms[to] = scaled.astype(jnp.bfloat16)
        pl.when(to != b)(copy.start)

        @pl.when(to == b)
        def _():
            got_terms[b] = terms[to]

    def joined(stats, count):
        top = stats[0, 0]
        for n in range(1, count):
            top = jnp.maximum(top, stats[n, 0])
        total = jnp.zeros_like(top)
        for n in range(count):
            total += stats[n, 1] * jnp.exp(stats[n, 0] - top)
        return top, total

    def to_all(peers, stats, send, recv):
        for n, peer in enumerate(peers):
            move(stats.at[0], stats.at[n + 1], send.at[n], recv.at[n], peer)

    def from_all(peers, stats, send, recv):
        for n, peer in enumerate(peers):
            arrive(stats.at[n + 1], send.at[n], recv.at[n], peer)

    def near_to_far(close, far, send, recv, far_send, far_recv):
        from_all(near, close, send, recv)
        top, total = joined(close, 4)
        far[0, 0] = top
        far[0, 1] = total
        to_all(there, far, far_send, far_recv)

    def ratio_of(close, far, far_send, far_recv):
        from_all(there, far, far_send, far_recv)
        top, total = joined(far, 16)
        return jnp.exp(close[0, 0] - top) / total

    first_shared, late_shared, thin_shared = [], [], []
    first = [route(states, side, h, first_shared) for side in range(2)]
    late = [route(states, side, 1 - h, late_shared) for side in range(2)]
    thin = [route(slices, side, h, thin_shared) for side in range(2)]
    thin_late = [route(slices, side, 1 - h, thin_shared) for side in range(2)]

    def go(*groups):
        for group in groups:
            for r in group:
                next(r, None)

    across = step_of(states.at[y, h, x, c], {H: 1 - h}, states.at[y, 1 - h, x, c])
    for part in range(2):
        head_start(0, part)
    go(first)
    lax.fori_loop(0, 8, norm_student, 0)
    slices_start()
    go(first)
    go(first)
    head_next(1)
    slices_arrive()
    thin_across = step_of(slices.at[y, h, x, c], {H: 1 - h}, slices.at[y, 1 - h, x, c])
    go(first, thin)
    across()
    go(late, first)
    head_next(2)
    go(late, thin)
    own_teacher_head.wait()
    for wait in first_shared:
        wait()
    teach(0, h)
    teach(1, h)
    go(late)
    head_next(3)
    teach(2, h)
    teach(3, h)
    go(late, thin)
    thin_across()
    go(thin_late)
    head_next(4)
    go(late, thin)
    for wait in late_shared:
        wait()
    head_next(5)
    for row in range(4):
        teach(row, 1 - h)
    to_all(near, near_stats, near_send, near_recv)
    go(thin, thin_late)
    head_next(6)
    near_to_far(near_stats, far_stats, near_send, near_recv, far_send, far_recv)
    go(thin_late)
    for part in range(2):
        head_arrive(6, part)
    own_head.wait()

    def add_block(q, total):
        columns = normed[:, pl.ds(pl.multiple_of(q * 512, 512), 512)]
        return total + lax.dot_general(
            heads[q], columns, (((1,), (1,)), ((), ())), preferred_element_type=jnp.float32
        )

    logits = lax.fori_loop(0, 8, add_block, jnp.zeros((320, 128), jnp.float32))
    local_top = jnp.max(logits, axis=0, keepdims=True)
    scaled = jnp.exp(logits - local_top)
    near_student[0, 0] = jnp.broadcast_to(local_top, (8, 128))
    near_student[0, 1] = jnp.broadcast_to(jnp.sum(scaled, axis=0, keepdims=True), (8, 128))
    to_all(near, near_student, student_near_send, student_near_recv)
    factor[...] = ratio_of(near_stats, far_stats, far_send, far_recv) * (
        weight_ref[...].astype(jnp.float32) / DEN
    )
    got_factor[b] = factor[...]
    spread(lambda at: factor, got_factor, factor_send, factor_recv)
    go(thin_late)
    near_to_far(near_student, far_student, student_near_send, student_near_recv, student_far_send, student_far_recv)
    go(thin_late)
    for wait in thin_shared:
        wait()
    for at in range(8):
        for n in range(4):
            joined_slices[at, :, 128 * n : 128 * n + 128] = slices[
                :, :, n, at // 4, :, 128 * (at % 4) : 128 * (at % 4) + 128
            ].reshape(128, 128)
    own_ratio = ratio_of(near_student, far_student, student_far_send, student_far_recv)[0:1]
    collect(got_factor, factor_send, factor_recv)
    for n in range(8):
        waits = remote(got_terms.at[n], got_terms.at[n], term_send.at[n], term_recv.at[n], along[0])
        pl.when(b != n)(waits.wait_recv)

    def add_branch(n, mixed):
        return mixed + got_terms[n].astype(jnp.float32) * got_factor[n, pl.ds(b, 1), :]

    mixed = lax.fori_loop(0, 8, add_branch, jnp.zeros((320, 128), jnp.float32))
    place = ((2 * y + h) * 4 + x) * 2 + c
    entries = lax.broadcasted_iota(jnp.int32, (320, 128), 0) + 320 * place
    onehot = (entries == label_ref[...]).astype(jnp.float32)
    targets = (1.0 - mix_label) * mixed + mix_label * onehot
    all_grads[b] = (loss_scale * (scaled * own_ratio - targets)).astype(jnp.bfloat16)

    low = 4 * (b // 4)
    mates = [low + ring(slot, step, 4) for step in range(1, 4)]
    sources = [low + ring(slot, -step, 4) for step in range(1, 4)]
    partner = ring(b, 4, 8)
    move(all_grads.at[b], all_grads.at[b], grad_send.at[3], grad_recv.at[3], {B: partner})
    for n, mate in enumerate(mates):
        move(all_grads.at[b], all_grads.at[b], grad_send.at[n], grad_recv.at[n], {B: mate})

    def part(q):
        result = lax.dot_general(
            all_grads[b], heads[q], (((0,), (0,)), ((), ())), preferred_element_type=jnp.float32
        )
        columns = pl.ds(pl.multiple_of(q * 512, 512), 512)
        weighted = hidden_ref[:, columns].astype(jnp.float32) * gain_ref[:, columns]
        return result, jnp.sum(result * weighted, axis=1, keepdims=True)

    column_dots = jnp.zeros((128, 1), jnp.float32)
    for n in range(4):
        result, dot = part(2 * n + (1 - c))
        give_part[n] = result
        column_dots += dot
        move(give_part.at[n], got_part.at[n], part_send.at[n], part_recv.at[n], {C: 1 - c})
    for n in range(4):
        result, dot = part(2 * n + c)
        own_part[n] = result
        column_dots += dot
    dots[0] = jnp.broadcast_to(column_dots, (128, 128)).T[0:8]
    for n, peer in enumerate(there):
        move(dots.at[0], dots_far.at[n], dots_send.at[n], dots_recv.at[n], peer)
    for dy in range(4):
        row = ring(y, dy, 4)
        arrive(got_part.at[row], part_send.at[row], part_recv.at[row], {C: 1 - c})
        both = own_part[row] + got_part[row]
        for m in range(4):
            plane_give[row, m] = both[:, 128 * m : 128 * m + 128].astype(jnp.bfloat16)
        for n, peer in enumerate(there):
            if plane[n][0] == dy:
                move(plane_give.at[row, peer[X]], plane_got.at[n], plane_send.at[n], plane_recv.at[n], peer)

    def pass_on():
        arrive(all_grads.at[partner], grad_send.at[3], grad_recv.at[3], {B: partner})
        for n, mate in enumerate(mates):
            move(all_grads.at[partner], all_grads.at[partner], grad_send.at[4 + n], grad_recv.at[4 + n], {B: mate})

    def add_head(at):
        grad_head_ref[...] += jnp.dot(all_grads[at], joined_slices[at], preferred_element_type=jnp.float32)

    row_dots = dots[0]
    for n, peer in enumerate(there):
        arrive(dots_far.at[n], dots_send.at[n], dots_recv.at[n], peer)
        row_dots += dots_far[n]
    dots_near[0] = row_dots
    to_all(near, dots_near, dot_near_send, dot_near_recv)
    pass_on()
    block = plane_give[y, x].astype(jnp.float32)
    for n, peer in enumerate(there):
        arrive(plane_got.at[n], plane_send.at[n], plane_recv.at[n], peer)
        block += plane_got[n].astype(jnp.float32)
    chip_cols = pl.ds(pl.multiple_of(128 * ((2 * y + c) * 4 + x), 128), 128)
    summands = block * hidden_ref[:, chip_cols].astype(jnp.float32) * inv_cols[...]
    sums[...] = jnp.broadcast_to(jnp.sum(summands, axis=0, keepdims=True), (8, 128))
    own_slot = 2 * b + h
    turned = block.T
    piece[0] = turned[0:64]
    piece[1] = turned[64:128]
    half_copies = [
        remote(piece.at[core], halves.at[h], half_send.at[core], half_recv.at[h], {H: c, C: core}) for core in range(2)
    ]
    for core, copy in enumerate(half_copies):
        mine = jnp.logical_and(h == c, c == core)
        pl.when(jnp.logical_not(mine))(copy.start)

        @pl.when(mine)
        def _():
            halves[h] = piece[core]

    sum_copies = [
        (step, core, remote(
            sums, got_sums.at[own_slot], sum_send.at[step, core], sum_recv.at[own_slot],
            {B: ring(b, step, 8), H: c, C: core},
        ))
        for step in range(8) for core in range(2)
    ]
    stays = h == c
    for step, core, copy in sum_copies:
        if step:
            copy.start()
        else:
            pl.when(jnp.logical_not(jnp.logical_and(stays, c == core)))(copy.start)

    @pl.when(stays)
    def _():
        got_sums[own_slot] = sums[...]

    grad_head_ref[...] = jnp.dot(all_grads[b], joined_slices[b], preferred_element_type=jnp.float32)
    add_head(partner)
    from_all(near, dots_near, dot_near_send, dot_near_recv)
    row_dot = (dots_near[0] + dots_near[1] + dots_near[2] + dots_near[3])[0:1]
    for source in range(2):
        waits = remote(
            halves.at[source], halves.at[source], half_send.at[0], half_recv.at[source], {C: 1 - c}
        )
        pl.when(jnp.logical_not(jnp.logical_and(h == source, c == h)))(waits.wait_recv)
    normed_grads = halves[0] + halves[1]
    inv_scale = inv_cols[...].T[0:1]
    own_cols = pl.ds(pl.multiple_of(128 * ((2 * y + h) * 4 + x), 128), 128)
    chip[0] = hidden_ref[:, own_cols].astype(jnp.float32).T
    chip[1] = jnp.broadcast_to(gain_ref[:, own_cols], (128, 128)).T
    own_rows = pl.ds(pl.multiple_of(64 * c, 64), 64)
    values, gain_cols = chip[0, own_rows, :], chip[1, own_rows, :]
    hidden_out_ref[...] = (
        inv_scale * gain_cols * normed_grads - values * inv_scale**3 * row_dot / width_of_model
    )
    for n, source in enumerate(sources):
        arrive(all_grads.at[source], grad_send.at[n], grad_recv.at[n], {B: partner})
        add_head(source)
    for n, source in enumerate(sources):
        other = ring(source, 4, 8)
        arrive(all_grads.at[other], grad_send.at[4 + n], grad_recv.at[4 + n], {B: partner})
        add_head(other)
    for n in range(16):
        waits = remote(got_sums.at[n], got_sums.at[n], sum_send.at[0, 0], sum_recv.at[n], along[0])
        pl.when(jnp.logical_not(jnp.logical_and(stays, own_slot == n)))(waits.wait_recv)
    gain = got_sums[0]
    for n in range(1, 16):
        gain += got_sums[n]
    gain_out_ref[...] = jnp.where(c == 0, gain, jnp.concatenate([gain[:, 64:], gain[:, :64]], axis=1))

    for step, core, copy in sum_copies:
        if step:
            copy.wait_send()
        else:
            pl.when(jnp.logical_not(jnp.logical_and(stays, c == core)))(copy.wait_send)
    for copy in sent:
        copy.wait_send()
    for step in range(7):
        for part_number in range(2):
            head_sent(step, part_number)

    @pl.when(gives)
    def _():
        for copy in slice_copies:
            copy.wait_send()

    for n in range(8):
        _, copy = term_copy(n // 2, n % 2)
        pl.when(b != n)(copy.wait_send)
    for core, copy in enumerate(half_copies):
        pl.when(jnp.logical_not(jnp.logical_and(h == c, c == core)))(copy.wait_send)


def run(*operands):
    inside = pl.BlockSpec(memory_space=pltpu.VMEM)
    anywhere = pl.BlockSpec(memory_space=pl.ANY)
    f32, bf16 = jnp.float32, jnp.bfloat16
    dma = pltpu.SemaphoreType.DMA
    arrays = [
        ((4, 2, 4, 2, 16, 4096), bf16), ((320, 4096), bf16), ((8, 320, 512), bf16), ((128, 4096), bf16),
        ((4, 2, 4, 2, 16, 512), bf16), ((8, 128, 512), bf16), ((128, 128), f32),
        ((8, 320, 128), bf16), ((8, 320, 128), bf16), ((4, 2, 8, 128), f32), ((16, 2, 8, 128), f32),
        ((4, 2, 8, 128), f32), ((16, 2, 8, 128), f32), ((8, 128), f32), ((8, 8, 128), f32), ((8, 320, 128), bf16),
        ((4, 128, 512), f32), ((4, 128, 512), f32), ((4, 128, 512), f32), ((4, 4, 128, 128), bf16),
        ((15, 128, 128), bf16), ((1, 8, 128), f32), ((4, 8, 128), f32), ((15, 8, 128), f32),
        ((2, 64, 128), f32), ((2, 64, 128), f32), ((8, 128), f32), ((16, 8, 128), f32), ((2, 128, 128), f32),
    ]
    counts = [(128,), (2, 7, 2), None, (8,), (3,), (15,), (3,), (15,), (7,), (7,), (4,), (15,), (15,), (3,), (2,)]
    semaphores = [dma((3,))]
    for count in counts:
        semaphores += [dma((7,)), dma((4,))] if count is None else [dma(count), dma(count)]
    semaphores += [dma((8, 2)), dma((16,))]
    return pl.pallas_call(
        kernel,
        out_shape=(
            jax.ShapeDtypeStruct((320, 512), f32),
            jax.ShapeDtypeStruct((64, 128), f32),
            jax.ShapeDtypeStruct((8, 128), f32),
        ),
        in_specs=[inside, inside, anywhere, inside, inside, anywhere, inside, inside],
        out_specs=(inside,) * 3,
        scratch_shapes=[pltpu.VMEM(*array) for array in arrays] + semaphores,
        compiler_params=pltpu.CompilerParams(collective_id=0, has_side_effects=True, vmem_limit_bytes=56 << 20),
        name="distill",
    )(*operands)


def per_device(
    teacher_hidden, teacher_gain, teacher_head, student_hidden, student_gain, student_head, cluster_weights, token_ids
):
    grad_head, grad_hidden, grad_gain = run(
        teacher_hidden[0], teacher_gain, teacher_head[0].T, student_hidden, student_gain[None, :], student_head.T,
        cluster_weights.reshape(8, 128), token_ids[None, :],
    )
    return (grad_head.T, grad_hidden.T, grad_gain[0, :64])


def solution(mesh):
    split = Mesh(mesh.devices.reshape(mesh.shape["branch"], 4, 2, 4, 2), (B, *TOK))
    in_specs = (
        P("branch", TOK, None), P("branch", None), P("branch", None, TOK), P("branch", None), P(),
        P("branch", TOK), P(None, "branch"), P("branch"),
    )
    out_specs = (P("branch", TOK), P("branch", TOK), P(TOK))
    return jax.shard_map(per_device, mesh=split, in_specs=in_specs, out_specs=out_specs, check_vma=False)
```

```python
import jax
import jax.numpy as jnp
from jax import lax
from jax.experimental import pallas as pl
from jax.experimental.pallas import tpu as pltpu
from jax.sharding import Mesh
from jax.sharding import PartitionSpec as P

DEN = 64
eps = 1e-05
mix_label = 0.25
loss_scale = 64.0
width_of_model = 4096
MESH = pl.DeviceIdType.MESH
B, Y, H, X, C = "branch", "tok_0", "tok_1", "tok_2", "tok_3"
TOK = (Y, H, X, C)


def ring(value, step, size):
    return lax.rem(value + (step + size), size)


def kernel(
    hidden_block_ref, teacher_gain_ref, teacher_head_ref, hidden_ref, gain_ref, head_ref,
    weight_ref, label_ref,
    grad_head_ref, hidden_out_ref, gain_out_ref,
    states, head_cols, heads, normed, slices, joined_slices, inv_cols,
    terms, got_terms, near_stats, far_stats, near_student, far_student, factor, got_factor, all_grads,
    own_part, give_part, got_part, plane_give, plane_got, dots, dots_near, dots_far, piece, halves, sums, got_sums, chip,
    local_sem, send_sem, recv_sem, head_send, head_recv, piece_send, piece_recv,
    term_send, term_recv, near_send, near_recv, far_send, far_recv,
    student_near_send, student_near_recv, student_far_send, student_far_recv, factor_send, factor_recv,
    grad_send, grad_recv, part_send, part_recv, plane_send, plane_recv, dots_send, dots_recv,
    dot_near_send, dot_near_recv, half_send, half_recv, sum_send, sum_recv,
):
    b = lax.axis_index(B)
    y, h, x, c = (lax.axis_index(name) for name in TOK)
    along = [{B: ring(b, step, 8)} for step in range(1, 8)]
    near = [{H: h, C: 1 - c}, {H: 1 - h, C: c}, {H: 1 - h, C: 1 - c}]
    plane = [(dy, dx) for dy in range(4) for dx in range(4) if dy or dx]
    there = [{Y: ring(y, dy, 4), X: ring(x, dx, 4)} for dy, dx in plane]

    barrier = pltpu.get_barrier_semaphore()
    column = [
        {B: ring(b, step, 8), H: ring(h, dh, 2), C: ring(c, dc, 2)}
        for step in range(8) for dh in range(2) for dc in range(2) if step or dh or dc
    ]
    for peer in column + there:
        pl.semaphore_signal(barrier, inc=1, device_id=peer, device_id_type=MESH)
    own_teacher_head = pltpu.make_async_copy(teacher_head_ref, head_cols, local_sem.at[0])
    own_teacher_head.start()
    own_head = pltpu.make_async_copy(head_ref, heads.at[b], local_sem.at[1])
    own_head.start()

    def unit_rows(hidden, gain):
        values = hidden.astype(jnp.float32)
        inv_scale = lax.rsqrt(jnp.mean(values * values, axis=-1, keepdims=True) + eps)
        return (values * inv_scale * gain).astype(jnp.bfloat16), inv_scale

    states[y, h, x, c] = unit_rows(hidden_block_ref[...], teacher_gain_ref[...])[0]
    def norm_student(n, carry):
        rows = pl.ds(pl.multiple_of(16 * n, 16), 16)
        unit, inv_scale = unit_rows(hidden_ref[rows, :], gain_ref[...])
        normed[rows, :] = unit
        inv_cols[rows, :] = jnp.broadcast_to(inv_scale, (16, 128))
        return carry

    lax.fori_loop(0, 8, norm_student, 0)
    pl.semaphore_wait(barrier, len(column) + len(there))

    numbers = iter(range(128))
    sent = []

    def remote(source, target, send, recv, peer):
        return pltpu.make_async_remote_copy(
            src_ref=source, dst_ref=target, send_sem=send, recv_sem=recv, device_id=peer, device_id_type=MESH
        )

    def move(source, target, send, recv, peer):
        copy = remote(source, target, send, recv, peer)
        copy.start()
        sent.append(copy)

    def arrive(target, send, recv, peer):
        remote(target, target, send, recv, peer).wait_recv()

    def step_of(part, peer, arriving):
        number = next(numbers)
        send, recv = send_sem.at[number], recv_sem.at[number]
        move(part, part, send, recv, peer)
        return remote(arriving, arriving, send, recv, peer).wait_recv

    def spread(source_of, target, send, recv):
        for n, peer in enumerate(along):
            move(source_of(peer[B]), target.at[b], send.at[n], recv.at[n], peer)

    def collect(target, send, recv):
        for n in range(7):
            arrive(target.at[ring(b, -(n + 1), 8)], send.at[n], recv.at[n], along[n])

    def route(ref, side, layer, shared):
        half = ref.shape[-1] // 2
        start = side * half
        cols = pl.ds(start, half)
        quarters = (pl.ds(start, half // 2), pl.ds(start + half // 2, half // 2))
        axis, other = ((X, Y), (Y, X))[side]
        mine, theirs = ((x, y), (y, x))[side]
        every = pl.ds(0, 4)

        def beside(step, cs):
            at = ring(mine, step, 4)
            return ref.at[y, layer, at, c, :, cs] if side == 0 else ref.at[at, layer, x, c, :, cs]

        def rows(step, core, cs):
            at = ring(theirs, step, 4)
            return ref.at[at, layer, every, core, :, cs] if side == 0 else ref.at[every, layer, at, core, :, cs]

        def share(step):
            shared.append(step_of(rows(step, c, cols), {C: 1 - c}, rows(step, 1 - c, cols)))

        forth, back = {axis: ring(mine, 1, 4)}, {axis: ring(mine, -1, 4)}
        up = step_of(beside(0, cols), forth, beside(-1, cols))
        down = step_of(beside(0, cols), back, beside(1, cols))
        yield
        up()
        far_up = step_of(beside(-1, quarters[0]), forth, beside(2, quarters[0]))
        down()
        far_down = step_of(beside(1, quarters[1]), back, beside(2, quarters[1]))
        yield
        far_up()
        far_down()
        forth, back = {other: ring(theirs, 1, 4)}, {other: ring(theirs, -1, 4)}
        up = step_of(rows(0, c, cols), forth, rows(-1, c, cols))
        down = step_of(rows(0, c, cols), back, rows(1, c, cols))
        share(0)
        yield
        up()
        far_up = step_of(rows(-1, c, quarters[0]), forth, rows(2, c, quarters[0]))
        down()
        far_down = step_of(rows(1, c, quarters[1]), back, rows(2, c, quarters[1]))
        share(-1)
        share(1)
        yield
        far_up()
        far_down()
        share(2)

    def head_copies(step, part):
        rows = pl.ds(80 * part, 80)
        low, high = jnp.maximum(b - step, 0), jnp.minimum(b + step, 7)
        up = remote(
            (head_ref if step == 0 else heads.at[low]).at[rows], heads.at[low, rows],
            head_send.at[0, step, part], head_recv.at[0, step, part], {B: jnp.minimum(b + 1, 7)},
        )
        down = remote(
            (head_ref if step == 0 else heads.at[high]).at[rows], heads.at[high, rows],
            head_send.at[1, step, part], head_recv.at[1, step, part], {B: jnp.maximum(b - 1, 0)},
        )
        return (
            (up, jnp.logical_and(b < 7, b >= step), b >= step + 1),
            (down, jnp.logical_and(b > 0, b + step <= 7), b + step <= 6),
        )

    def head_start(step, part):
        for copy, sends, _ in head_copies(step, part):
            pl.when(sends)(copy.start)

    def head_arrive(step, part):
        for copy, _, receives in head_copies(step, part):
            pl.when(receives)(copy.wait_recv)

    def head_sent(step, part):
        for copy, sends, _ in head_copies(step, part):
            pl.when(sends)(copy.wait_send)

    def head_next(step):
        for part in range(4):
            head_arrive(step - 1, part)
            head_start(step, part)

    slot = lax.rem(b, 4)
    gives = (b // 4) == c
    part_rows = pl.ds(pl.multiple_of(16 * (2 * y + h), 16), 16)

    def slice_part(at):
        return normed.at[part_rows, pl.ds(pl.multiple_of(512 * at + 128 * x, 128), 128)]

    def slice_at(number):
        return slices.at[y, h, x, c, :, pl.ds(pl.multiple_of(128 * number, 128), 128)]

    slice_copies = [
        remote(slice_part(peer[B]), slice_at(slot), piece_send.at[n], piece_recv.at[slot], peer)
        for n, peer in enumerate(along)
    ]
    own_slice = pltpu.make_async_copy(slice_part(b), slice_at(slot), local_sem.at[2])

    def slices_start():
        @pl.when(gives)
        def _():
            own_slice.start()
            for copy in slice_copies:
                copy.start()

    def slices_arrive():
        for number in range(4):
            arriving = remote(slice_at(number), slice_at(number), piece_send.at[0], piece_recv.at[number], along[0])
            pl.when(b != 4 * c + number)(arriving.wait_recv)
        pl.when(gives)(own_slice.wait)

    def term_copy(row, layer):
        to = 2 * row + layer
        return to, remote(terms.at[to], got_terms.at[b], term_send.at[to], term_recv.at[b], {B: to})

    def teach(row, layer):
        to = 2 * row + layer

        def add_columns(k, total):
            columns = pl.ds(pl.multiple_of(1024 * k, 1024), 1024)
            return total + lax.dot_general(
                head_cols[:, columns], states[row, layer, :, :, :, columns].reshape(128, 1024),
                (((1,), (1,)), ((), ())), preferred_element_type=jnp.float32,
            )

        logits = lax.fori_loop(0, 4, add_columns, jnp.zeros((320, 128), jnp.float32))
        top = jnp.max(logits, axis=0, keepdims=True)
        scaled = jnp.exp(logits - top)
        near_stats[0, 0, pl.ds(to, 1), :] = top
        near_stats[0, 1, pl.ds(to, 1), :] = jnp.sum(scaled, axis=0, keepdims=True)
        terms[to] = scaled.astype(jnp.bfloat16)
        @pl.when(to == b)
        def _():
            got_terms[b] = terms[to]

    def terms_start():
        for number in range(8):
            _, copy = term_copy(number // 2, number % 2)
            pl.when(b != number)(copy.start)

    def joined(stats, count):
        top = stats[0, 0]
        for n in range(1, count):
            top = jnp.maximum(top, stats[n, 0])
        total = jnp.zeros_like(top)
        for n in range(count):
            total += stats[n, 1] * jnp.exp(stats[n, 0] - top)
        return top, total

    def to_all(peers, stats, send, recv):
        for n, peer in enumerate(peers):
            move(stats.at[0], stats.at[n + 1], send.at[n], recv.at[n], peer)

    def from_all(peers, stats, send, recv):
        for n, peer in enumerate(peers):
            arrive(stats.at[n + 1], send.at[n], recv.at[n], peer)

    def near_to_far(close, far, send, recv, far_send, far_recv):
        from_all(near, close, send, recv)
        top, total = joined(close, 4)
        far[0, 0] = top
        far[0, 1] = total
        to_all(there, far, far_send, far_recv)

    def ratio_of(close, far, far_send, far_recv):
        from_all(there, far, far_send, far_recv)
        top, total = joined(far, 16)
        return jnp.exp(close[0, 0] - top) / total

    first_shared, late_shared, thin_shared = [], [], []
    first = [route(states, side, h, first_shared) for side in range(2)]
    late = [route(states, side, 1 - h, late_shared) for side in range(2)]
    thin = [route(slices, side, h, thin_shared) for side in range(2)]
    thin_late = [route(slices, side, 1 - h, thin_shared) for side in range(2)]

    def go(*groups):
        for group in groups:
            for r in group:
                next(r, None)

    across = step_of(states.at[y, h, x, c], {H: 1 - h}, states.at[y, 1 - h, x, c])
    for part in range(4):
        head_start(0, part)
    go(first)
    slices_start()
    go(first)
    go(first)
    head_next(1)
    slices_arrive()
    thin_across = step_of(slices.at[y, h, x, c], {H: 1 - h}, slices.at[y, 1 - h, x, c])
    go(first, thin)
    across()
    go(late, first)
    head_next(2)
    go(late, thin)
    own_teacher_head.wait()
    for wait in first_shared:
        wait()
    teach(0, h)
    teach(1, h)
    go(late)
    head_next(3)
    teach(2, h)
    teach(3, h)
    go(late, thin)
    thin_across()
    go(thin_late)
    head_next(4)
    go(late, thin)
    for wait in late_shared:
        wait()
    head_next(5)
    for row in range(4):
        teach(row, 1 - h)
    to_all(near, near_stats, near_send, near_recv)
    terms_start()
    go(thin, thin_late)
    head_next(6)
    near_to_far(near_stats, far_stats, near_send, near_recv, far_send, far_recv)
    go(thin_late)
    for part in range(4):
        head_arrive(6, part)
    own_head.wait()

    def add_block(q, total):
        columns = normed[:, pl.ds(pl.multiple_of(q * 512, 512), 512)]
        return total + lax.dot_general(
            heads[q], columns, (((1,), (1,)), ((), ())), preferred_element_type=jnp.float32
        )

    logits = lax.fori_loop(0, 8, add_block, jnp.zeros((320, 128), jnp.float32))
    local_top = jnp.max(logits, axis=0, keepdims=True)
    scaled = jnp.exp(logits - local_top)
    near_student[0, 0] = jnp.broadcast_to(local_top, (8, 128))
    near_student[0, 1] = jnp.broadcast_to(jnp.sum(scaled, axis=0, keepdims=True), (8, 128))
    to_all(near, near_student, student_near_send, student_near_recv)
    factor[...] = ratio_of(near_stats, far_stats, far_send, far_recv) * (
        weight_ref[...].astype(jnp.float32) / DEN
    )
    got_factor[b] = factor[...]
    spread(lambda at: factor, got_factor, factor_send, factor_recv)
    go(thin_late)
    near_to_far(near_student, far_student, student_near_send, student_near_recv, student_far_send, student_far_recv)
    go(thin_late)
    for wait in thin_shared:
        wait()
    for at in range(8):
        for n in range(4):
            joined_slices[at, :, 128 * n : 128 * n + 128] = slices[
                :, :, n, at // 4, :, 128 * (at % 4) : 128 * (at % 4) + 128
            ].reshape(128, 128)
    own_ratio = ratio_of(near_student, far_student, student_far_send, student_far_recv)[0:1]
    collect(got_factor, factor_send, factor_recv)
    for n in range(8):
        waits = remote(got_terms.at[n], got_terms.at[n], term_send.at[n], term_recv.at[n], along[0])
        pl.when(b != n)(waits.wait_recv)

    def add_branch(n, mixed):
        return mixed + got_terms[n].astype(jnp.float32) * got_factor[n, pl.ds(b, 1), :]

    mixed = lax.fori_loop(0, 8, add_branch, jnp.zeros((320, 128), jnp.float32))
    place = ((2 * y + h) * 4 + x) * 2 + c
    entries = lax.broadcasted_iota(jnp.int32, (320, 128), 0) + 320 * place
    onehot = (entries == label_ref[...]).astype(jnp.float32)
    targets = (1.0 - mix_label) * mixed + mix_label * onehot
    all_grads[b] = (loss_scale * (scaled * own_ratio - targets)).astype(jnp.bfloat16)

    low = 4 * (b // 4)
    mates = [low + ring(slot, step, 4) for step in range(1, 4)]
    sources = [low + ring(slot, -step, 4) for step in range(1, 4)]
    partner = ring(b, 4, 8)
    move(all_grads.at[b], all_grads.at[b], grad_send.at[3], grad_recv.at[3], {B: partner})
    for n, mate in enumerate(mates):
        move(all_grads.at[b], all_grads.at[b], grad_send.at[n], grad_recv.at[n], {B: mate})

    def part(q):
        result = lax.dot_general(
            all_grads[b], heads[q], (((0,), (0,)), ((), ())), preferred_element_type=jnp.float32
        )
        columns = pl.ds(pl.multiple_of(q * 512, 512), 512)
        weighted = hidden_ref[:, columns].astype(jnp.float32) * gain_ref[:, columns]
        return result, jnp.sum(result * weighted, axis=1, keepdims=True)

    column_dots = jnp.zeros((128, 1), jnp.float32)
    for n in range(4):
        result, dot = part(2 * n + (1 - c))
        give_part[n] = result
        column_dots += dot
        move(give_part.at[n], got_part.at[n], part_send.at[n], part_recv.at[n], {C: 1 - c})
    for n in range(4):
        result, dot = part(2 * n + c)
        own_part[n] = result
        column_dots += dot
    dots[0] = jnp.broadcast_to(column_dots, (128, 128)).T[0:8]
    for n, peer in enumerate(there):
        move(dots.at[0], dots_far.at[n], dots_send.at[n], dots_recv.at[n], peer)
    for dy in range(4):
        row = ring(y, dy, 4)
        arrive(got_part.at[row], part_send.at[row], part_recv.at[row], {C: 1 - c})
        both = own_part[row] + got_part[row]
        for m in range(4):
            plane_give[row, m] = both[:, 128 * m : 128 * m + 128].astype(jnp.bfloat16)
        for n, peer in enumerate(there):
            if plane[n][0] == dy:
                move(plane_give.at[row, peer[X]], plane_got.at[n], plane_send.at[n], plane_recv.at[n], peer)

    def pass_on():
        arrive(all_grads.at[partner], grad_send.at[3], grad_recv.at[3], {B: partner})
        for n, mate in enumerate(mates):
            move(all_grads.at[partner], all_grads.at[partner], grad_send.at[4 + n], grad_recv.at[4 + n], {B: mate})

    def add_head(at):
        grad_head_ref[...] += jnp.dot(all_grads[at], joined_slices[at], preferred_element_type=jnp.float32)

    row_dots = dots[0]
    for n, peer in enumerate(there):
        arrive(dots_far.at[n], dots_send.at[n], dots_recv.at[n], peer)
        row_dots += dots_far[n]
    dots_near[0] = row_dots
    to_all(near, dots_near, dot_near_send, dot_near_recv)
    pass_on()
    block = plane_give[y, x].astype(jnp.float32)
    for n, peer in enumerate(there):
        arrive(plane_got.at[n], plane_send.at[n], plane_recv.at[n], peer)
        block += plane_got[n].astype(jnp.float32)
    chip_cols = pl.ds(pl.multiple_of(128 * ((2 * y + c) * 4 + x), 128), 128)
    summands = block * hidden_ref[:, chip_cols].astype(jnp.float32) * inv_cols[...]
    sums[...] = jnp.broadcast_to(jnp.sum(summands, axis=0, keepdims=True), (8, 128))
    own_slot = 2 * b + h
    turned = block.T
    piece[0] = turned[0:64]
    piece[1] = turned[64:128]
    half_copies = [
        remote(piece.at[core], halves.at[h], half_send.at[core], half_recv.at[h], {H: c, C: core}) for core in range(2)
    ]
    for core, copy in enumerate(half_copies):
        mine = jnp.logical_and(h == c, c == core)
        pl.when(jnp.logical_not(mine))(copy.start)

        @pl.when(mine)
        def _():
            halves[h] = piece[core]

    sum_copies = [
        (step, core, remote(
            sums, got_sums.at[own_slot], sum_send.at[step, core], sum_recv.at[own_slot],
            {B: ring(b, step, 8), H: c, C: core},
        ))
        for step in range(8) for core in range(2)
    ]
    stays = h == c
    for step, core, copy in sum_copies:
        if step:
            copy.start()
        else:
            pl.when(jnp.logical_not(jnp.logical_and(stays, c == core)))(copy.start)

    @pl.when(stays)
    def _():
        got_sums[own_slot] = sums[...]

    grad_head_ref[...] = jnp.dot(all_grads[b], joined_slices[b], preferred_element_type=jnp.float32)
    add_head(partner)
    from_all(near, dots_near, dot_near_send, dot_near_recv)
    row_dot = (dots_near[0] + dots_near[1] + dots_near[2] + dots_near[3])[0:1]
    for source in range(2):
        waits = remote(
            halves.at[source], halves.at[source], half_send.at[0], half_recv.at[source], {C: 1 - c}
        )
        pl.when(jnp.logical_not(jnp.logical_and(h == source, c == h)))(waits.wait_recv)
    normed_grads = halves[0] + halves[1]
    inv_scale = inv_cols[...].T[0:1]
    own_cols = pl.ds(pl.multiple_of(128 * ((2 * y + h) * 4 + x), 128), 128)
    chip[0] = hidden_ref[:, own_cols].astype(jnp.float32).T
    chip[1] = jnp.broadcast_to(gain_ref[:, own_cols], (128, 128)).T
    own_rows = pl.ds(pl.multiple_of(64 * c, 64), 64)
    values, gain_cols = chip[0, own_rows, :], chip[1, own_rows, :]
    hidden_out_ref[...] = (
        inv_scale * gain_cols * normed_grads - values * inv_scale**3 * row_dot / width_of_model
    )
    for n, source in enumerate(sources):
        arrive(all_grads.at[source], grad_send.at[n], grad_recv.at[n], {B: partner})
        add_head(source)
    for n, source in enumerate(sources):
        other = ring(source, 4, 8)
        arrive(all_grads.at[other], grad_send.at[4 + n], grad_recv.at[4 + n], {B: partner})
        add_head(other)
    for n in range(16):
        waits = remote(got_sums.at[n], got_sums.at[n], sum_send.at[0, 0], sum_recv.at[n], along[0])
        pl.when(jnp.logical_not(jnp.logical_and(stays, own_slot == n)))(waits.wait_recv)
    gain = got_sums[0]
    for n in range(1, 16):
        gain += got_sums[n]
    gain_out_ref[...] = jnp.where(c == 0, gain, jnp.concatenate([gain[:, 64:], gain[:, :64]], axis=1))

    for step, core, copy in sum_copies:
        if step:
            copy.wait_send()
        else:
            pl.when(jnp.logical_not(jnp.logical_and(stays, c == core)))(copy.wait_send)
    for copy in sent:
        copy.wait_send()
    for step in range(7):
        for part_number in range(4):
            head_sent(step, part_number)

    @pl.when(gives)
    def _():
        for copy in slice_copies:
            copy.wait_send()

    for n in range(8):
        _, copy = term_copy(n // 2, n % 2)
        pl.when(b != n)(copy.wait_send)
    for core, copy in enumerate(half_copies):
        pl.when(jnp.logical_not(jnp.logical_and(h == c, c == core)))(copy.wait_send)


def run(*operands):
    inside = pl.BlockSpec(memory_space=pltpu.VMEM)
    anywhere = pl.BlockSpec(memory_space=pl.ANY)
    f32, bf16 = jnp.float32, jnp.bfloat16
    dma = pltpu.SemaphoreType.DMA
    arrays = [
        ((4, 2, 4, 2, 16, 4096), bf16), ((320, 4096), bf16), ((8, 320, 512), bf16), ((128, 4096), bf16),
        ((4, 2, 4, 2, 16, 512), bf16), ((8, 128, 512), bf16), ((128, 128), f32),
        ((8, 320, 128), bf16), ((8, 320, 128), bf16), ((4, 2, 8, 128), f32), ((16, 2, 8, 128), f32),
        ((4, 2, 8, 128), f32), ((16, 2, 8, 128), f32), ((8, 128), f32), ((8, 8, 128), f32), ((8, 320, 128), bf16),
        ((4, 128, 512), f32), ((4, 128, 512), f32), ((4, 128, 512), f32), ((4, 4, 128, 128), bf16),
        ((15, 128, 128), bf16), ((1, 8, 128), f32), ((4, 8, 128), f32), ((15, 8, 128), f32),
        ((2, 64, 128), f32), ((2, 64, 128), f32), ((8, 128), f32), ((16, 8, 128), f32), ((2, 128, 128), f32),
    ]
    counts = [(128,), (2, 7, 4), None, (8,), (3,), (15,), (3,), (15,), (7,), (7,), (4,), (15,), (15,), (3,), (2,)]
    semaphores = [dma((3,))]
    for count in counts:
        semaphores += [dma((7,)), dma((4,))] if count is None else [dma(count), dma(count)]
    semaphores += [dma((8, 2)), dma((16,))]
    return pl.pallas_call(
        kernel,
        out_shape=(
            jax.ShapeDtypeStruct((320, 512), f32),
            jax.ShapeDtypeStruct((64, 128), f32),
            jax.ShapeDtypeStruct((8, 128), f32),
        ),
        in_specs=[inside, inside, anywhere, inside, inside, anywhere, inside, inside],
        out_specs=(inside,) * 3,
        scratch_shapes=[pltpu.VMEM(*array) for array in arrays] + semaphores,
        compiler_params=pltpu.CompilerParams(collective_id=0, has_side_effects=True, vmem_limit_bytes=56 << 20),
        name="distill",
    )(*operands)


def per_device(
    teacher_hidden, teacher_gain, teacher_head, student_hidden, student_gain, student_head, cluster_weights, token_ids
):
    grad_head, grad_hidden, grad_gain = run(
        teacher_hidden[0], teacher_gain, teacher_head[0].T, student_hidden, student_gain[None, :], student_head.T,
        cluster_weights.reshape(8, 128), token_ids[None, :],
    )
    return (grad_head.T, grad_hidden.T, grad_gain[0, :64])


def solution(mesh):
    split = Mesh(mesh.devices.reshape(mesh.shape["branch"], 4, 2, 4, 2), (B, *TOK))
    in_specs = (
        P("branch", TOK, None), P("branch", None), P("branch", None, TOK), P("branch", None), P(),
        P("branch", TOK), P(None, "branch"), P("branch"),
    )
    out_specs = (P("branch", TOK), P("branch", TOK), P(TOK))
    return jax.shard_map(per_device, mesh=split, in_specs=in_specs, out_specs=out_specs, check_vma=False)
```
